256 devices in a mesh: grp: 8 (over z_lo, core), seq: 32 (over z_hi, y, x).
Axes of the slice: x: 4, y: 4, z: 8 (z_hi: 2, z_lo: 4; z = z_hi * 4 + z_lo), core: 2. Of those that a mesh axis runs over, the one named last changes fastest.
Arguments:
- q_resp: bfloat16 [8, 8192, 1280], P('grp', 'seq'), may hold values from -5 to 5
- resp_kv: bfloat16 [8, 8192, 512], P('grp', 'seq'), may hold values from -5 to 5
- prompt_kv: bfloat16 [8, 1024, 512], P(None, ('grp', 'seq')), may hold values from -5 to 5
- d_out: bfloat16 [8, 8192, 1280], P('grp', 'seq'), may hold values from -5 to 5
- resp_lengths: int32 [8, 32, 4], P('grp', 'seq'), may hold values from 1 to 128, 256 in all within a row
Outputs:
- attn_out: bfloat16 [8, 8192, 1280], P('grp', 'seq')
- d_query: bfloat16 [8, 8192, 1280], P('grp', 'seq')
- d_resp_kv: bfloat16 [8, 8192, 512], P('grp', 'seq')
- d_prompt_kv: bfloat16 [8, 1024, 512], P(None, ('grp', 'seq'))
The draws below stay inside these ranges and needn't reach their ends.
Inputs may be any that keep to these rules, and one draw needn't show every extreme that they name: `resp_lengths`: on each device the lengths sum to 256; the longest response of a device has 128 tokens on some device.
All inputs are finite; a program needn't handle non-finite values.
Results may differ from the reference program's by a relative error of at most 0.03.
Values may be sent and summed in bfloat16 or wider, within the bound.
No kernel may reach another device: no remote copies, remote signals or barrier semaphores. Data moves between devices by JAX's collectives and lax.ppermute only.
A program may use at most 64 MiB of HBM per device.

```python
import math
import jax
import jax.numpy as jnp
import numpy as np
from jax import lax

HEADS = 10
KV_HEADS = 2
HEAD = 128
SLOTS = 4
ROWS_DEV = 256
GROUPS = 8
PROMPT = 1024
ROWS = 8192
N_SEQ = 32


def draw_prompt_kv(key, part):
    key = jax.random.fold_in(key, 11)
    values = jnp.clip(jax.random.normal(key, (GROUPS, PROMPT, 2 * KV_HEADS * HEAD), jnp.float32), -5.0, 5.0)
    return values.astype(jnp.bfloat16)


def draw_q_resp(key, part):
    key = jax.random.fold_in(key, 23)
    values = jnp.clip(jax.random.normal(key, (GROUPS, ROWS, HEADS * HEAD), jnp.float32), -5.0, 5.0)
    return values.astype(jnp.bfloat16)


def block_levels(stream_key, extent, pieces, low, largest):
    level = 1.0
    for axis_at, parts in pieces:
        heights = jax.random.uniform(jax.random.fold_in(jax.random.fold_in(stream_key, 6), axis_at), (parts,), jnp.float32, low / len(pieces), largest / len(pieces))
        level = level * jnp.repeat(jnp.exp(heights), extent[axis_at] // parts).reshape((-1,) + (1,) * (len(extent) - 1 - axis_at))
    return level


def split_up(number_of, total, bound, slope):
    portions = [(1 << 20) // math.isqrt(grade ** slope) + 1 for grade in range(2, number_of + 1)]
    rest, counts = total - bound - (number_of - 1), [1] * (number_of - 1)
    while rest > 0:
        movable = [i for i in range(number_of - 1) if counts[i] < bound]
        whole, remaining = sum([portions[i] for i in movable]), rest
        for i in movable:
            extra = min(bound - counts[i], max(1, remaining * portions[i] // whole), rest)
            counts[i] = counts[i] + extra
            rest = rest - extra
    return np.array([bound] + counts)


def uneven(rng, number_of, total, most, slope):
    if number_of == 2:
        one = jax.random.randint(rng, (), max(1, total - most), min(most, total - 1) + 1)
        return jnp.stack([one, total - one])
    tallies = jnp.asarray(split_up(number_of, total, most, slope), jnp.int32)
    twos = (number_of - 1) // 2
    giver, taker = tallies[1:1 + 2 * twos:2], tallies[2:2 + 2 * twos:2]
    margin = jnp.minimum(giver - 1, most - taker)
    moved = jax.random.randint(jax.random.fold_in(rng, 1), (twos,), 0, 1 << 20) % (margin + 1)
    tallies = tallies.at[1:1 + 2 * twos:2].set(giver - moved).at[2:2 + 2 * twos:2].set(taker + moved)
    return tallies[jax.random.permutation(jax.random.fold_in(rng, 2), number_of)]


def gaussian(rng, shape, spread, bound, shards=(), kind=jnp.bfloat16):
    values = jax.random.normal(rng, shape, jnp.float32) * spread
    if len(shards) > 0:
        values = block_levels(rng, shape, shards, -0.22, 0.18) * values
    return jnp.clip(values, min=-bound, max=bound).astype(kind)


def setup_inputs(seed: int = 0) -> dict:
    key_list = jax.random.split(jax.random.key(seed), 6)
    q_resp = draw_q_resp(jax.random.fold_in(key_list[5], 71), 0)
    resp_kv = gaussian(key_list[1], (GROUPS, ROWS, 2 * KV_HEADS * HEAD), 1.0, 5.0, ((0, 8), (1, 32)))
    prompt_kv = draw_prompt_kv(jax.random.fold_in(key_list[5], 71), 0)
    d_out = gaussian(key_list[3], (GROUPS, ROWS, HEADS * HEAD), 1.0, 5.0, ((0, 8), (1, 32)))
    resp_lengths = jax.vmap(lambda own: uneven(own, SLOTS, ROWS_DEV, ROWS_DEV // 2, 2))(jax.random.split(key_list[4], GROUPS * N_SEQ)).reshape((GROUPS, N_SEQ, SLOTS)).astype(jnp.int32)
    return dict(q_resp=q_resp, resp_kv=resp_kv, prompt_kv=prompt_kv, d_out=d_out, resp_lengths=resp_lengths)


def segment_ids(lens, rows):
    ends = jnp.cumsum(lens)
    places = jnp.arange(rows, dtype=jnp.int32)
    return jnp.sum((places[:, None] >= ends[None, :]).astype(jnp.int32), axis=1)


def block_grads(queries, resp_pair, prompt_pair, grads_out, lens):
    rows = queries.shape[0]
    width = KV_HEADS * HEAD
    repeat = HEADS // KV_HEADS
    scale = HEAD ** -0.5
    seg = segment_ids(lens, rows)
    places = jnp.arange(rows, dtype=jnp.int32)
    self_ok = (seg[:, None] == seg[None, :]) & (places[None, :] <= places[:, None])
    allowed = jnp.concatenate([jnp.ones((rows, PROMPT), dtype=bool), self_ok], axis=1)
    keys_all = jnp.concatenate([prompt_pair[:, :width], resp_pair[:, :width]], 0).reshape(-1, KV_HEADS, HEAD)
    vals_all = jnp.concatenate([prompt_pair[:, width:], resp_pair[:, width:]], 0).reshape(-1, KV_HEADS, HEAD)
    query4 = queries.reshape(rows, KV_HEADS, repeat, HEAD)
    grad4 = grads_out.reshape(rows, KV_HEADS, repeat, HEAD)
    keys32 = keys_all.astype(jnp.float32)
    vals32 = vals_all.astype(jnp.float32)
    query32 = query4.astype(jnp.float32)
    grad32 = grad4.astype(jnp.float32)
    scores = jnp.einsum("rgnd,jgd->gnrj", query32, keys32) * scale
    scores = jnp.where(allowed[None, None], scores, -jnp.inf)
    top = jnp.max(scores, axis=-1, keepdims=True)
    weights = jnp.exp(scores - top)
    probs = weights / jnp.sum(weights, axis=-1, keepdims=True)
    probs_low = probs.astype(jnp.bfloat16)
    attn = jnp.einsum("gnrj,jgd->rgnd", probs_low.astype(jnp.float32), vals32).astype(jnp.bfloat16)
    delta = jnp.sum(grad32 * attn.astype(jnp.float32), axis=-1).transpose(1, 2, 0)
    d_probs = jnp.einsum("rgnd,jgd->gnrj", grad32, vals32)
    d_scores = (probs * (d_probs - delta[..., None])).astype(jnp.bfloat16)
    d_scores32 = d_scores.astype(jnp.float32)
    d_query = (scale * jnp.einsum("gnrj,jgd->rgnd", d_scores32, keys32)).astype(jnp.bfloat16)
    d_keys = scale * jnp.einsum("gnrj,rgnd->jgd", d_scores32, query32)
    d_vals = jnp.einsum("gnrj,rgnd->jgd", probs_low.astype(jnp.float32), grad32)
    d_pair = jnp.concatenate([d_keys.reshape(-1, width), d_vals.reshape(-1, width)], 1)
    return (attn.reshape(rows, HEADS * HEAD), d_query.reshape(rows, HEADS * HEAD),
            d_pair[PROMPT:].astype(jnp.bfloat16), d_pair[:PROMPT])


def reference(q_resp, resp_kv, prompt_kv, d_out, resp_lengths):
    blocks = resp_lengths.shape[1]

    def one_group(items):
        queries, resp_pair, prompt_pair, grads_out, lens = items
        rows = queries.shape[0] // blocks

        def step(total, block):
            q_blk, kv_blk, g_blk, l_blk = block
            attn, d_query, d_self, d_prompt = block_grads(q_blk, kv_blk, prompt_pair, g_blk, l_blk)
            return total + d_prompt, (attn, d_query, d_self)

        start = jnp.zeros((PROMPT, 2 * KV_HEADS * HEAD), jnp.float32)
        total, outs = lax.scan(step, start, (queries.reshape(blocks, rows, -1), resp_pair.reshape(blocks, rows, -1), grads_out.reshape(blocks, rows, -1), lens))
        return outs[0].reshape(blocks * rows, -1), outs[1].reshape(blocks * rows, -1), outs[2].reshape(blocks * rows, -1), total.astype(jnp.bfloat16)

    attn_out, d_query, d_resp_kv, d_prompt_kv = lax.map(one_group, (q_resp, resp_kv, prompt_kv, d_out, resp_lengths))
    return attn_out, d_query, d_resp_kv, d_prompt_kv
```

```python
import functools

import jax
import jax.numpy as jnp
from jax import lax
from jax.experimental import pallas as pl
from jax.experimental.pallas import tpu as pltpu
from jax.sharding import Mesh
from jax.sharding import PartitionSpec as P

HEADS = 10
KV_HEADS = 2
HEAD = 128
REPEAT = HEADS // KV_HEADS
SCALE = HEAD ** (-0.5)
LOG2E = 1.4426950408889634
MASKED = -1e30
bf16 = jnp.bfloat16
f32 = jnp.float32
ALONG_X = 4


def dot_nn(a, b):
    return lax.dot_general(a, b, (((1,), (0,)), ((), ())), preferred_element_type=f32)


def dot_nt(a, b):
    return lax.dot_general(a, b, (((1,), (1,)), ((), ())), preferred_element_type=f32)


def self_bias(lens_ref, rows):
    key = lax.broadcasted_iota(jnp.int32, (rows, rows), 0)
    row = lax.broadcasted_iota(jnp.int32, (rows, rows), 1)
    key_seg = jnp.zeros((rows, rows), jnp.int32)
    row_seg = jnp.zeros((rows, rows), jnp.int32)
    end = jnp.int32(0)
    for i in range(lens_ref.shape[-1]):
        end = end + lens_ref[0, 0, i]
        key_seg += (key >= end).astype(jnp.int32)
        row_seg += (row >= end).astype(jnp.int32)
    return jnp.where((key_seg == row_seg) & (key <= row), 0.0, MASKED).astype(f32)


def attention_kernel(has_earlier, lens_ref, q_ref, do_ref, resp_k_ref, resp_v_ref, *refs):
    parts = refs[:ALONG_X]
    refs = refs[ALONG_X:]
    if has_earlier:
        earlier_self, refs = refs[0], refs[3:]
    attn_ref, dq_ref, d_self_ref = refs[:3]
    d_parts = refs[3 : 3 + ALONG_X]
    bias_ref, k_t, v_t, acc = refs[3 + ALONG_X :]
    rows = q_ref.shape[1]
    step = pl.program_id(0)
    span = parts[0].shape[0]
    total = ALONG_X * span

    @pl.when(step == 0)
    def _():
        bias_ref[...] = self_bias(lens_ref, rows)
        for i, part in enumerate(parts):
            k_t[:, i * span : (i + 1) * span] = part[:, :HEAD].T
            v_t[:, i * span : (i + 1) * span] = part[:, HEAD:].T
        k_t[:, total:] = resp_k_ref[0].T
        v_t[:, total:] = resp_v_ref[0].T

    q_t = q_ref[0].T
    do_t = do_ref[0].T
    keys = [part[:, :HEAD] for part in parts] + [resp_k_ref[0]]
    vals = [part[:, HEAD:] for part in parts] + [resp_v_ref[0]]
    places = [slice(i * span, (i + 1) * span) for i in range(ALONG_X)] + [slice(total, total + rows)]
    scores = [dot_nn(k, q_t) for k in keys]
    scores[-1] = scores[-1] + bias_ref[...]
    top = functools.reduce(
        jnp.maximum, [jnp.max(s, axis=0, keepdims=True) for s in scores]
    ) * (SCALE * LOG2E)
    weights = [jnp.exp2(s * (SCALE * LOG2E) - top) for s in scores]
    inverse = 1.0 / sum(jnp.sum(w, axis=0, keepdims=True) for w in weights)
    low = [w.astype(bf16) for w in weights]
    out_t = sum(dot_nn(v_t[:, at], w) for at, w in zip(places, low)) * inverse
    attn_ref[0] = out_t.T.astype(bf16)
    delta = jnp.sum(do_t.astype(f32) * out_t.astype(bf16).astype(f32), axis=0, keepdims=True)
    d_scores = [
        (w * (dot_nn(v, do_t) - delta)).astype(bf16) for v, w in zip(vals, weights)
    ]
    dq_t = sum(dot_nn(k_t[:, at], d) for at, d in zip(places, d_scores)) * (inverse * SCALE)
    dq_ref[0] = dq_t.T.astype(bf16)
    q_scaled = (q_t.astype(f32) * (inverse * SCALE)).astype(bf16)
    do_scaled = (do_t.astype(f32) * inverse).astype(bf16)

    def add(first):
        for i, (mine, theirs) in enumerate(((q_scaled, d_scores), (do_scaled, low))):
            for at, t in zip(places, theirs):
                new = dot_nt(mine, t)
                acc[i, :, at] = new if first else acc[i, :, at] + new

    @pl.when(step == 0)
    def _():
        add(True)

    @pl.when(step > 0)
    def _():
        add(False)

    @pl.when(step == REPEAT - 1)
    def _():
        for i in range(2):
            cols = slice(i * HEAD, (i + 1) * HEAD)
            for at, d_part in zip(places, d_parts):
                d_part[:, cols] = acc[i, :, at].T.astype(bf16)
            if has_earlier:
                d_self_ref[0, :, 2 * i * HEAD : (2 * i + 1) * HEAD] = earlier_self[0, :, cols]
                d_self_ref[0, :, (2 * i + 1) * HEAD : (2 * i + 2) * HEAD] = acc[
                    i, :, total:
                ].T.astype(bf16)
            else:
                d_self_ref[0, :, cols] = acc[i, :, total:].T.astype(bf16)


def attention(head, lens, q, do, resp, parts, earlier):
    rows = q.shape[1]
    span = parts[0].shape[0]
    keys = ALONG_X * span + rows
    block = lambda place: pl.BlockSpec((1, rows, HEAD), lambda h, p=place: (0, 0, p(h)))
    whole = lambda *shape: pl.BlockSpec(shape, lambda h: (0,) * len(shape))
    of_head = lambda h: head * REPEAT + h
    pair = whole(span, 2 * HEAD)
    has_earlier = earlier is not None
    in_specs = [
        pl.BlockSpec(memory_space=pltpu.SMEM),
        block(of_head),
        block(of_head),
        block(lambda h: head),
        block(lambda h: KV_HEADS + head),
    ] + [pair] * ALONG_X
    args = [lens, q, do, resp, resp, *parts]
    width = 2 * HEAD
    aliases = {}
    if has_earlier:
        width = 2 * KV_HEADS * HEAD
        attn, dq, d_self = earlier
        in_specs += [whole(1, rows, 2 * HEAD)] + [pl.BlockSpec(memory_space=pl.ANY)] * 2
        aliases = {len(args) + 1: 0, len(args) + 2: 1}
        args += [d_self, attn, dq]
    full = jax.ShapeDtypeStruct((1, rows, HEADS * HEAD), bf16)
    out = pl.pallas_call(
        functools.partial(attention_kernel, has_earlier),
        grid=(REPEAT,),
        in_specs=in_specs,
        out_specs=[block(of_head), block(of_head), whole(1, rows, width)] + [pair] * ALONG_X,
        out_shape=[full, full, jax.ShapeDtypeStruct((1, rows, width), bf16)]
        + [jax.ShapeDtypeStruct((span, 2 * HEAD), bf16)] * ALONG_X,
        scratch_shapes=[
            pltpu.VMEM((rows, rows), f32),
            pltpu.VMEM((HEAD, keys), bf16),
            pltpu.VMEM((HEAD, keys), bf16),
            pltpu.VMEM((2, HEAD, keys), f32),
        ],
        input_output_aliases=aliases,
        compiler_params=pltpu.CompilerParams(vmem_limit_bytes=32 << 20),
        cost_estimate=pl.CostEstimate(
            flops=12 * REPEAT * rows * keys * HEAD,
            bytes_accessed=4 << 20,
            transcendentals=REPEAT * rows * keys,
        ),
        name=f"attention_{head}",
    )(*args)
    return out[:3], out[3:]


def shifted(by):
    return [(i, (i + by) % ALONG_X) for i in range(ALONG_X)]


def on_device(q_resp, resp_kv, prompt_kv, d_out, resp_lengths):
    groups, own_rows, width = prompt_kv.shape
    ring = ("zl", "c", "zh", "y")
    copies = lax.axis_size("zh") * lax.axis_size("y")
    mine = prompt_kv.reshape(groups, own_rows, 2, KV_HEADS, HEAD).transpose(0, 3, 1, 2, 4)
    mine = mine.reshape(groups, 1, KV_HEADS, own_rows, 2 * HEAD)
    sent = jnp.broadcast_to(mine, (groups, copies) + mine.shape[2:])
    sent = sent.reshape((groups * copies,) + mine.shape[2:])
    got = lax.all_to_all(sent, ring, split_axis=0, concat_axis=0, tiled=True)
    got = got.transpose(1, 0, 2, 3).reshape(KV_HEADS, -1, 2 * HEAD)
    earlier = None
    sums = []
    pairs = []
    for head in range(KV_HEADS):
        own = got[head]
        pairs.append([own] + [lax.ppermute(own, "x", shifted(-by)) for by in (1, 3, 2)])
    for head in range(KV_HEADS):
        earlier, partial = attention(
            head, resp_lengths, q_resp, d_out, resp_kv, pairs[head], earlier
        )
        back = [partial[0]] + [
            lax.ppermute(t, "x", shifted(by)) for t, by in zip(partial[1:], (1, 3, 2))
        ]
        sums.append(sum(t.astype(f32) for t in back).astype(bf16))
    attn, dq, d_self = earlier
    total = jnp.stack(sums).reshape(KV_HEADS, groups * copies, own_rows, 2 * HEAD)
    total = lax.all_to_all(
        total.transpose(1, 0, 2, 3), ring, split_axis=0, concat_axis=0, tiled=True
    )
    total = total.reshape(groups, copies, KV_HEADS, own_rows, 2, HEAD)
    d_prompt = jnp.sum(total.astype(f32), axis=1).astype(bf16)
    d_prompt = d_prompt.transpose(0, 2, 3, 1, 4).reshape(groups, own_rows, width)
    return attn, dq, d_self, d_prompt


def solution(mesh):
    fine = Mesh(mesh.devices.reshape(4, 2, 2, 4, 4), ("zl", "c", "zh", "y", "x"))
    grp, seq = ("zl", "c"), ("zh", "y", "x")
    rows = P(grp, seq, None)
    prompt = P(None, grp + seq, None)
    return jax.shard_map(
        on_device,
        mesh=fine,
        in_specs=(rows, rows, prompt, rows, rows),
        out_specs=(rows, rows, rows, prompt),
        check_vma=False,
    )
```

```python
import functools

import jax
import jax.numpy as jnp
from jax import lax
from jax.experimental import pallas as pl
from jax.experimental.pallas import tpu as pltpu
from jax.sharding import Mesh
from jax.sharding import PartitionSpec as P

HEADS = 10
KV_HEADS = 2
HEAD = 128
REPEAT = HEADS // KV_HEADS
SCALE = HEAD ** (-0.5)
LOG2E = 1.4426950408889634
MASKED = -1e30
bf16 = jnp.bfloat16
f32 = jnp.float32
ALONG_X = 4


def dot_nn(a, b):
    return lax.dot_general(a, b, (((1,), (0,)), ((), ())), preferred_element_type=f32)


def dot_nt(a, b):
    return lax.dot_general(a, b, (((1,), (1,)), ((), ())), preferred_element_type=f32)


def self_bias(lens_ref, rows):
    key = lax.broadcasted_iota(jnp.int32, (rows, rows), 0)
    row = lax.broadcasted_iota(jnp.int32, (rows, rows), 1)
    key_seg = jnp.zeros((rows, rows), jnp.int32)
    row_seg = jnp.zeros((rows, rows), jnp.int32)
    end = jnp.int32(0)
    for i in range(lens_ref.shape[-1]):
        end = end + lens_ref[0, 0, i]
        key_seg += (key >= end).astype(jnp.int32)
        row_seg += (row >= end).astype(jnp.int32)
    return jnp.where((key_seg == row_seg) & (key <= row), 0.0, MASKED).astype(f32)


def attention_kernel(has_earlier, lens_ref, q_ref, do_ref, resp_k_ref, resp_v_ref, *refs):
    parts = refs[:ALONG_X]
    refs = refs[ALONG_X:]
    if has_earlier:
        earlier_self, refs = refs[0], refs[3:]
    attn_ref, dq_ref, d_self_ref = refs[:3]
    d_parts = refs[3 : 3 + ALONG_X]
    bias_ref, k_t, v_t, acc, scores_ref, low_ref, d_probs_ref = refs[3 + ALONG_X :]
    rows = q_ref.shape[1]
    span = parts[0].shape[0]
    total = ALONG_X * span
    places = [slice(i * span, (i + 1) * span) for i in range(ALONG_X)] + [slice(total, total + rows)]
    keys = [part[:, :HEAD] for part in parts] + [resp_k_ref[0]]
    vals = [part[:, HEAD:] for part in parts] + [resp_v_ref[0]]
    last = len(keys) - 1
    bias_ref[...] = self_bias(lens_ref, rows)
    for at, k, v in zip(places, keys, vals):
        k_t[:, at] = k.T
        v_t[:, at] = v.T
    state = [{} for _ in range(REPEAT)]

    def over_keys(op, t):
        return op(t.reshape(t.shape[0] // 8, 8, rows), axis=0)

    def score_pass(h):
        q_t = q_ref[0, :, h * HEAD : (h + 1) * HEAD].T
        tops = []
        for i, (at, k) in enumerate(zip(places, keys)):
            s = dot_nn(k, q_t)
            if i == last:
                s = s + bias_ref[...]
            scores_ref[h % 2, at, :] = s
            tops.append(over_keys(jnp.max, s))
        top = jnp.max(functools.reduce(jnp.maximum, tops), axis=0, keepdims=True)
        state[h].update(q_t=q_t, top=top * (SCALE * LOG2E))

    def forward_pass(h):
        cols = slice(h * HEAD, (h + 1) * HEAD)
        top = state[h]["top"]
        do_t = do_ref[0, :, cols].T
        sums, out_t = [], 0.0
        for at, v in zip(places, vals):
            w = jnp.exp2(scores_ref[h % 2, at, :] * (SCALE * LOG2E) - top)
            sums.append(over_keys(jnp.sum, w))
            low = w.astype(bf16)
            low_ref[h % 2, at, :] = low
            d_probs_ref[h % 2, at, :] = dot_nn(v, do_t)
            out_t = out_t + dot_nn(v_t[:, at], low)
        inverse = 1.0 / jnp.sum(sum(sums), axis=0, keepdims=True)
        out_t = out_t * inverse
        attn_ref[0, :, cols] = out_t.T.astype(bf16)
        delta = jnp.sum(
            do_t.astype(f32) * out_t.astype(bf16).astype(f32), axis=0, keepdims=True
        )
        state[h].update(do_t=do_t, inverse=inverse, delta=delta)

    def backward_pass(h):
        inverse, delta = state[h]["inverse"], state[h]["delta"]
        q_scaled = (state[h]["q_t"].astype(f32) * (inverse * SCALE)).astype(bf16)
        do_scaled = (state[h]["do_t"].astype(f32) * inverse).astype(bf16)
        dq_t = 0.0
        for at in places:
            low = low_ref[h % 2, at, :]
            d_scores = (low.astype(f32) * (d_probs_ref[h % 2, at, :] - delta)).astype(bf16)
            dq_t = dq_t + dot_nn(k_t[:, at], d_scores)
            for j, (mine, theirs) in enumerate(((q_scaled, d_scores), (do_scaled, low))):
                new = dot_nt(mine, theirs)
                acc[j, :, at] = new if h == 0 else acc[j, :, at] + new
        dq_ref[0, :, h * HEAD : (h + 1) * HEAD] = (dq_t * (inverse * SCALE)).T.astype(bf16)

    score_pass(0)
    for h in range(REPEAT):
        forward_pass(h)
        if h + 1 < REPEAT:
            score_pass(h + 1)
        backward_pass(h)
    for j in range(2):
        cols = slice(j * HEAD, (j + 1) * HEAD)
        for at, d_part in zip(places, d_parts):
            d_part[:, cols] = acc[j, :, at].T.astype(bf16)
        own = acc[j, :, total:].T.astype(bf16)
        if has_earlier:
            d_self_ref[0, :, 2 * j * HEAD : (2 * j + 1) * HEAD] = earlier_self[0, :, cols]
            d_self_ref[0, :, (2 * j + 1) * HEAD : (2 * j + 2) * HEAD] = own
        else:
            d_self_ref[0, :, cols] = own


def attention(head, lens, q, do, resp, parts, earlier):
    rows = q.shape[1]
    span = parts[0].shape[0]
    keys = ALONG_X * span + rows
    block = lambda n, at: pl.BlockSpec((1, rows, n), lambda i: (0, 0, at))
    whole = lambda *shape: pl.BlockSpec(shape, lambda i: (0,) * len(shape))
    of_heads = block(REPEAT * HEAD, head)
    pair = whole(span, 2 * HEAD)
    has_earlier = earlier is not None
    in_specs = [
        pl.BlockSpec(memory_space=pltpu.SMEM),
        of_heads,
        of_heads,
        block(HEAD, head),
        block(HEAD, KV_HEADS + head),
    ] + [pair] * ALONG_X
    args = [lens, q, do, resp, resp, *parts]
    width = 2 * HEAD
    aliases = {}
    if has_earlier:
        width = 2 * KV_HEADS * HEAD
        attn, dq, d_self = earlier
        in_specs += [whole(1, rows, 2 * HEAD)] + [pl.BlockSpec(memory_space=pl.ANY)] * 2
        aliases = {len(args) + 1: 0, len(args) + 2: 1}
        args += [d_self, attn, dq]
    full = jax.ShapeDtypeStruct((1, rows, HEADS * HEAD), bf16)
    out = pl.pallas_call(
        functools.partial(attention_kernel, has_earlier),
        grid=(1,),
        in_specs=in_specs,
        out_specs=[of_heads, of_heads, whole(1, rows, width)] + [pair] * ALONG_X,
        out_shape=[full, full, jax.ShapeDtypeStruct((1, rows, width), bf16)]
        + [jax.ShapeDtypeStruct((span, 2 * HEAD), bf16)] * ALONG_X,
        scratch_shapes=[
            pltpu.VMEM((rows, rows), f32),
            pltpu.VMEM((HEAD, keys), bf16),
            pltpu.VMEM((HEAD, keys), bf16),
            pltpu.VMEM((2, HEAD, keys), f32),
            pltpu.VMEM((2, keys, rows), f32),
            pltpu.VMEM((2, keys, rows), bf16),
            pltpu.VMEM((2, keys, rows), f32),
        ],
        input_output_aliases=aliases,
        compiler_params=pltpu.CompilerParams(vmem_limit_bytes=32 << 20),
        cost_estimate=pl.CostEstimate(
            flops=12 * REPEAT * rows * keys * HEAD,
            bytes_accessed=4 << 20,
            transcendentals=REPEAT * rows * keys,
        ),
        name=f"attention_{head}",
    )(*args)
    return out[:3], out[3:]


def partner(by):
    return [(i, i ^ by) for i in range(ALONG_X)]


def on_device(q_resp, resp_kv, prompt_kv, d_out, resp_lengths):
    groups, own_rows, width = prompt_kv.shape
    ring = ("zl", "c", "zh", "y")
    copies = lax.axis_size("zh") * lax.axis_size("y")
    mine = prompt_kv.reshape(groups, own_rows, 2, KV_HEADS, HEAD).transpose(0, 3, 1, 2, 4)
    mine = mine.reshape(groups, 1, KV_HEADS, own_rows, 2 * HEAD)
    sent = jnp.broadcast_to(mine, (groups, copies) + mine.shape[2:])
    sent = sent.reshape((groups * copies,) + mine.shape[2:])
    got = lax.all_to_all(sent, ring, split_axis=0, concat_axis=0, tiled=True)
    got = got.transpose(1, 0, 2, 3).reshape(KV_HEADS, -1, 2 * HEAD)
    earlier = None
    sums = []
    pairs = []
    for head in range(KV_HEADS):
        own = got[head]
        pairs.append([own] + [lax.ppermute(own, "x", partner(by)) for by in (2, 1, 3)])
    for head in range(KV_HEADS):
        earlier, partial = attention(
            head, resp_lengths, q_resp, d_out, resp_kv, pairs[head], earlier
        )
        back = [partial[0]] + [
            lax.ppermute(t, "x", partner(by)) for t, by in zip(partial[1:], (2, 1, 3))
        ]
        sums.append(sum(t.astype(f32) for t in back).astype(bf16))
    attn, dq, d_self = earlier
    total = jnp.stack(sums).reshape(KV_HEADS, groups * copies, own_rows, 2 * HEAD)
    total = lax.all_to_all(
        total.transpose(1, 0, 2, 3), ring, split_axis=0, concat_axis=0, tiled=True
    )
    total = total.reshape(groups, copies, KV_HEADS, own_rows, 2, HEAD)
    d_prompt = jnp.sum(total.astype(f32), axis=1).astype(bf16)
    d_prompt = d_prompt.transpose(0, 2, 3, 1, 4).reshape(groups, own_rows, width)
    return attn, dq, d_self, d_prompt


def solution(mesh):
    fine = Mesh(mesh.devices.reshape(4, 2, 2, 4, 4), ("zl", "c", "zh", "y", "x"))
    grp, seq = ("zl", "c"), ("zh", "y", "x")
    rows = P(grp, seq, None)
    prompt = P(None, grp + seq, None)
    return jax.shard_map(
        on_device,
        mesh=fine,
        in_specs=(rows, rows, prompt, rows, rows),
        out_specs=(rows, rows, rows, prompt),
        check_vma=False,
    )
```

```python
import functools

import jax
import jax.numpy as jnp
from jax import lax
from jax.experimental import pallas as pl
from jax.experimental.pallas import tpu as pltpu
from jax.sharding import Mesh
from jax.sharding import PartitionSpec as P

HEADS = 10
KV_HEADS = 2
HEAD = 128
REPEAT = HEADS // KV_HEADS
SCALE = HEAD ** (-0.5)
LOG2E = 1.4426950408889634
MASKED = -1e30
PARTNERS = 3
SHIFTS = (2, 1, 3)
WIDTH = KV_HEADS * HEAD
bf16 = jnp.bfloat16
f32 = jnp.float32


def dot_nn(a, b):
    return lax.dot_general(a, b, (((1,), (0,)), ((), ())), preferred_element_type=f32)


def dot_nt(a, b):
    return lax.dot_general(a, b, (((1,), (1,)), ((), ())), preferred_element_type=f32)


def by_eights(op, t):
    return op(t.reshape(t.shape[0] // 8, 8, t.shape[1]), axis=0)


def of_keys(head):
    at = head // REPEAT * HEAD
    return slice(at, at + HEAD)


def of_vals(head):
    at = WIDTH + head // REPEAT * HEAD
    return slice(at, at + HEAD)


def of_head(head):
    return slice(head * HEAD, (head + 1) * HEAD)


def self_bias(lens_ref, rows):
    key = lax.broadcasted_iota(jnp.int32, (rows, rows), 0)
    row = lax.broadcasted_iota(jnp.int32, (rows, rows), 1)
    key_seg = jnp.zeros((rows, rows), jnp.int32)
    row_seg = jnp.zeros((rows, rows), jnp.int32)
    end = jnp.int32(0)
    for i in range(lens_ref.shape[-1]):
        end = end + lens_ref[0, 0, i]
        key_seg += (key >= end).astype(jnp.int32)
        row_seg += (row >= end).astype(jnp.int32)
    return jnp.where((key_seg == row_seg) & (key <= row), 0.0, MASKED).astype(f32)


def scaled(t, factor):
    return (t.astype(f32) * factor).astype(bf16)


def near_forward_kernel(
    lens_hbm, q_hbm, resp_hbm, own_ref, low_ref, out_ref, stat_ref,
    lens_ref, q_ref, resp_ref, bias_ref, scores_ref, arrived,
):
    rows, span = q_ref.shape[1], own_ref.shape[0]
    arriving = [
        pltpu.make_async_copy(source, target, arrived.at[i])
        for i, (source, target) in enumerate(
            ((lens_hbm, lens_ref), (resp_hbm, resp_ref), (q_hbm, q_ref))
        )
    ]
    for copy in arriving:
        copy.start()
    arriving[0].wait()
    bias_ref[...] = self_bias(lens_ref, rows)
    arriving[1].wait()
    arriving[2].wait()
    places = [slice(0, span), slice(span, span + rows)]
    vals_t = [
        (own_ref[:, of_vals(g * REPEAT)].T, resp_ref[0, :, of_vals(g * REPEAT)].T)
        for g in range(KV_HEADS)
    ]
    tops = {}

    def score_pass(h):
        q_t = q_ref[0, :, of_head(h)].T
        own = dot_nn(own_ref[:, of_keys(h)], q_t)
        resp = dot_nn(resp_ref[0, :, of_keys(h)], q_t) + bias_ref[...]
        scores_ref[h % 2, places[0]] = own
        scores_ref[h % 2, places[1]] = resp
        top = jnp.maximum(by_eights(jnp.max, own), by_eights(jnp.max, resp))
        tops[h] = jnp.max(top, axis=0, keepdims=True) * (SCALE * LOG2E)

    def forward_pass(h):
        sums, out_t = 0.0, 0.0
        for at, v_t in zip(places, vals_t[h // REPEAT]):
            weights = jnp.exp2(scores_ref[h % 2, at] * (SCALE * LOG2E) - tops[h])
            low = weights.astype(bf16)
            low_ref[h, at] = low
            sums = sums + by_eights(jnp.sum, weights)
            out_t = out_t + dot_nn(v_t, low)
        stat_ref[h, 0:8] = jnp.broadcast_to(tops[h], (8, rows))
        stat_ref[h, 8:16] = sums
        out_ref[h] = out_t.astype(bf16)

    score_pass(0)
    for h in range(HEADS):
        if h + 1 < HEADS:
            score_pass(h + 1)
        forward_pass(h)


def far_kernel(has_earlier, q_ref, do_ref, near_out_ref, near_stat_ref, *refs):
    pairs, refs = refs[:PARTNERS], refs[PARTNERS + has_earlier :]
    attn_ref, dq_ref, stat_ref = refs[:3]
    d_pairs, refs = refs[3 : 3 + PARTNERS], refs[3 + PARTNERS :]
    pair_t, acc, scores_ref, low_ref, d_probs_ref = refs
    rows, span = q_ref.shape[1], pairs[0].shape[0]
    places = [slice(i * span, (i + 1) * span) for i in range(PARTNERS)]
    for at, pair in zip(places, pairs):
        pair_t[:HEAD, at] = pair[:, :HEAD].T
        pair_t[HEAD:, at] = pair[:, HEAD:].T
    state = [{} for _ in range(REPEAT)]

    def score_pass(h):
        q_t = q_ref[0, :, of_head(h)].T
        tops = [near_stat_ref[h, 0:8]]
        for at, pair in zip(places, pairs):
            s = dot_nn(pair[:, :HEAD], q_t)
            scores_ref[h % 2, at] = s
            tops.append(by_eights(jnp.max, s) * (SCALE * LOG2E))
        top = jnp.max(functools.reduce(jnp.maximum, tops), axis=0, keepdims=True)
        state[h].update(q_t=q_t, top=top)

    def forward_pass(h):
        top = state[h]["top"]
        do_t = do_ref[0, :, of_head(h)].T
        before = jnp.exp2(near_stat_ref[h, 0:1] - top)
        sums = near_stat_ref[h, 8:16] * before
        out_t = near_out_ref[h].astype(f32) * before
        for at, pair in zip(places, pairs):
            w = jnp.exp2(scores_ref[h % 2, at] * (SCALE * LOG2E) - top)
            sums = sums + by_eights(jnp.sum, w)
            low = w.astype(bf16)
            low_ref[h % 2, at] = low
            d_probs_ref[h % 2, at] = dot_nn(pair[:, HEAD:], do_t)
            out_t = out_t + dot_nn(pair_t[HEAD:, at], low)
        inverse = 1.0 / jnp.sum(sums, axis=0, keepdims=True)
        out_t = out_t * inverse
        attn_ref[0, :, of_head(h)] = out_t.T.astype(bf16)
        delta = jnp.sum(
            do_t.astype(f32) * out_t.astype(bf16).astype(f32), axis=0, keepdims=True
        )
        stat_ref[h, 0:8] = jnp.broadcast_to(delta, (8, rows))
        stat_ref[h, 8:16] = jnp.broadcast_to(inverse * before, (8, rows))
        state[h].update(do_t=do_t, inverse=inverse, delta=delta)

    def backward_pass(h):
        inverse, delta = state[h]["inverse"], state[h]["delta"]
        q_scaled = scaled(state[h]["q_t"], inverse * SCALE)
        do_scaled = scaled(state[h]["do_t"], inverse)
        dq_t = 0.0
        for at in places:
            low = low_ref[h % 2, at]
            d_scores = (low.astype(f32) * (d_probs_ref[h % 2, at] - delta)).astype(bf16)
            dq_t = dq_t + dot_nn(pair_t[:HEAD, at], d_scores)
            for j, (mine, theirs) in enumerate(((q_scaled, d_scores), (do_scaled, low))):
                new = dot_nt(mine, theirs)
                acc[j, :, at] = new if h == 0 else acc[j, :, at] + new
        dq_ref[h] = (dq_t * (inverse * SCALE)).astype(bf16)

    score_pass(0)
    for h in range(REPEAT):
        forward_pass(h)
        if h + 1 < REPEAT:
            score_pass(h + 1)
        backward_pass(h)
    for at, d_pair in zip(places, d_pairs):
        d_pair[:, :HEAD] = acc[0, :, at].T.astype(bf16)
        d_pair[:, HEAD:] = acc[1, :, at].T.astype(bf16)


def near_backward_kernel(
    q_ref, do_ref, own_ref, resp_ref, low_ref, dq_0_ref, dq_1_ref, stat_0_ref, stat_1_ref,
    d_own_ref, d_resp_ref, dq_ref, acc, d_probs_ref,
):
    rows, span = q_ref.shape[1], own_ref.shape[0]
    places = [slice(0, span), slice(span, span + rows)]
    keys_t = [
        (own_ref[:, of_keys(g * REPEAT)].T, resp_ref[0, :, of_keys(g * REPEAT)].T)
        for g in range(KV_HEADS)
    ]
    d_outs = {}

    def d_probs_pass(h):
        d_outs[h] = do_ref[0, :, of_head(h)].T
        d_probs_ref[h % 2, places[0]] = dot_nn(own_ref[:, of_vals(h)], d_outs[h])
        d_probs_ref[h % 2, places[1]] = dot_nn(resp_ref[0, :, of_vals(h)], d_outs[h])

    def backward_pass(h):
        stat_ref, dq_part_ref = ((stat_0_ref, dq_0_ref), (stat_1_ref, dq_1_ref))[h // REPEAT]
        delta, share = stat_ref[h % REPEAT, 0:1], stat_ref[h % REPEAT, 8:9]
        q_scaled = scaled(q_ref[0, :, of_head(h)].T, share * SCALE)
        do_scaled = scaled(d_outs[h], share)
        dq_t = 0.0
        for at, k_t in zip(places, keys_t[h // REPEAT]):
            low = low_ref[h, at]
            d_scores = (low.astype(f32) * (d_probs_ref[h % 2, at] - delta)).astype(bf16)
            dq_t = dq_t + dot_nn(k_t, d_scores)
            for j, (mine, theirs) in enumerate(((q_scaled, d_scores), (do_scaled, low))):
                new = dot_nt(mine, theirs)
                acc[j, :, at] = new if h % REPEAT == 0 else acc[j, :, at] + new
        dq_t = dq_part_ref[h % REPEAT].astype(f32) + dq_t * (share * SCALE)
        dq_ref[0, :, of_head(h)] = dq_t.T.astype(bf16)
        if h % REPEAT == REPEAT - 1:
            for j, cols in enumerate((of_keys(h), of_vals(h))):
                d_own_ref[:, cols] = acc[j, :, places[0]].T
                d_resp_ref[0, :, cols] = acc[j, :, places[1]].T.astype(bf16)

    d_probs_pass(0)
    for h in range(HEADS):
        if h + 1 < HEADS:
            d_probs_pass(h + 1)
        backward_pass(h)


def whole(shape):
    return pl.BlockSpec(shape, lambda i: (0,) * len(shape))


def call(kernel, name, limit, outs, scratch, flops, exps, args, specs=(), out_specs=(), **kwargs):
    specs = list(specs) or [whole(t.shape) for t in args]
    return pl.pallas_call(
        kernel,
        grid=(1,),
        in_specs=specs,
        out_specs=list(out_specs) or [whole(shape) for shape, _ in outs],
        out_shape=[jax.ShapeDtypeStruct(shape, dtype) for shape, dtype in outs],
        scratch_shapes=[pltpu.VMEM(*t) if isinstance(t, tuple) else t for t in scratch],
        compiler_params=pltpu.CompilerParams(vmem_limit_bytes=limit << 20),
        cost_estimate=pl.CostEstimate(flops=flops, bytes_accessed=1 << 20, transcendentals=exps),
        name=name,
        **kwargs,
    )(*args)


def partner(by):
    return [(i, i ^ by) for i in range(PARTNERS + 1)]


def on_device(q_resp, resp_kv, prompt_kv, d_out, resp_lengths):
    groups, own_rows, width = prompt_kv.shape
    rows = q_resp.shape[1]
    ring = ("zl", "c", "zh", "y")
    copies = lax.axis_size(("zh", "y"))
    sent = jnp.broadcast_to(prompt_kv[:, None], (groups, copies, own_rows, width))
    sent = sent.reshape(-1, own_rows, width)
    own = lax.all_to_all(sent, ring, split_axis=0, concat_axis=0, tiled=True).reshape(-1, width)
    span = own.shape[0]
    near, far = span + rows, PARTNERS * span
    pairs = []
    for h in (0, REPEAT):
        pair = jnp.concatenate([own[:, of_keys(h)], own[:, of_vals(h)]], 1)
        pairs.append([lax.ppermute(pair, "x", partner(by)) for by in SHIFTS])

    flat, resp_kind = (q_resp.shape, bf16), (resp_kv.shape, bf16)
    product = 2 * rows * HEAD
    in_hbm = [pltpu.with_memory_space_constraint(t, pltpu.HBM) for t in (resp_lengths, q_resp, resp_kv)]
    low, near_out, near_stat = call(
        near_forward_kernel,
        "near_forward",
        16,
        [((HEADS, near, rows), bf16), ((HEADS, HEAD, rows), bf16), ((HEADS, 16, rows), f32)],
        [
            pltpu.SMEM(resp_lengths.shape, jnp.int32),
            pltpu.VMEM(q_resp.shape, bf16),
            pltpu.VMEM(resp_kv.shape, bf16),
            pltpu.VMEM((rows, rows), f32),
            pltpu.VMEM((2, near, rows), f32),
            pltpu.SemaphoreType.DMA((3,)),
        ],
        2 * HEADS * near * product,
        HEADS * near * rows,
        [*in_hbm, own],
        [pl.BlockSpec(memory_space=pltpu.HBM)] * 3 + [whole(own.shape)],
    )
    attn = None
    d_queries, stats, returned = [], [], []
    for g in range(KV_HEADS):
        of_group = pl.BlockSpec((1, rows, REPEAT * HEAD), lambda i, g=g: (0, 0, g))
        of_heads = lambda n, g=g: pl.BlockSpec((REPEAT, n, rows), lambda i: (g, 0, 0))
        pair_spec = whole((span, 2 * HEAD))
        specs = [of_group, of_group, of_heads(HEAD), of_heads(16)] + [pair_spec] * PARTNERS
        args = [q_resp, d_out, near_out, near_stat, *pairs[g]]
        if g:
            specs, args = specs + [pl.BlockSpec(memory_space=pl.ANY)], args + [attn]
        dq_kind, stat_kind = ((REPEAT, HEAD, rows), bf16), ((REPEAT, 16, rows), f32)
        attn, d_query, stat, *d_pairs = call(
            functools.partial(far_kernel, int(g > 0)),
            f"far_{g}",
            20,
            [flat, dq_kind, stat_kind] + [((span, 2 * HEAD), bf16)] * PARTNERS,
            [
                ((2 * HEAD, far), bf16),
                ((2, HEAD, far), f32),
                ((2, far, rows), f32),
                ((2, far, rows), bf16),
                ((2, far, rows), f32),
            ],
            6 * REPEAT * far * product,
            REPEAT * far * rows,
            args,
            specs,
            [of_group, whole(dq_kind[0]), whole(stat_kind[0])] + [pair_spec] * PARTNERS,
            input_output_aliases={len(args) - 1: 0} if g else {},
        )
        d_queries.append(d_query)
        stats.append(stat)
        if g:
            returned, d_pairs = lax.optimization_barrier((returned, d_pairs))
        returned.append([lax.ppermute(t, "x", partner(by)) for t, by in zip(d_pairs, SHIFTS)])
    d_own, d_resp, dq = call(
        near_backward_kernel,
        "near_backward",
        20,
        [(own.shape, f32), resp_kind, flat],
        [((2, HEAD, near), f32), ((2, near, rows), f32)],
        4 * HEADS * near * product,
        0,
        [q_resp, d_out, own, resp_kv, low, *d_queries, *stats],
    )
    total = [d_own[:, of_keys(0)], d_own[:, of_keys(REPEAT)], d_own[:, of_vals(0)], d_own[:, of_vals(REPEAT)]]
    for g in range(KV_HEADS):
        for t in returned[g]:
            total[g] = total[g] + t[:, :HEAD].astype(f32)
            total[KV_HEADS + g] = total[KV_HEADS + g] + t[:, HEAD:].astype(f32)
    total = jnp.concatenate(total, 1).astype(bf16).reshape(-1, own_rows, width)
    total = lax.all_to_all(total, ring, split_axis=0, concat_axis=0, tiled=True)
    total = total.reshape(groups, copies, own_rows, width)
    d_prompt = jnp.sum(total.astype(f32), axis=1).astype(bf16)
    return attn, dq, d_resp, d_prompt


def solution(mesh):
    fine = Mesh(mesh.devices.reshape(4, 2, 2, 4, 4), ("zl", "c", "zh", "y", "x"))
    grp, seq = ("zl", "c"), ("zh", "y", "x")
    rows = P(grp, seq, None)
    prompt = P(None, grp + seq, None)
    return jax.shard_map(
        on_device,
        mesh=fine,
        in_specs=(rows, rows, prompt, rows, rows),
        out_specs=(rows, rows, rows, prompt),
        check_vma=False,
    )
```

```python
import functools

import jax
import jax.numpy as jnp
from jax import lax
from jax.experimental import pallas as pl
from jax.experimental.pallas import tpu as pltpu
from jax.sharding import Mesh
from jax.sharding import PartitionSpec as P

HEADS = 10
KV_HEADS = 2
HEAD = 128
REPEAT = HEADS // KV_HEADS
SCALE = HEAD ** (-0.5)
LOG2E = 1.4426950408889634
MASKED = -1e30
WIDTH = KV_HEADS * HEAD
ROWS = 256
bf16 = jnp.bfloat16
f32 = jnp.float32


def dot_nn(a, b):
    return lax.dot_general(a, b, (((1,), (0,)), ((), ())), preferred_element_type=f32)


def dot_nt(a, b):
    return lax.dot_general(a, b, (((1,), (1,)), ((), ())), preferred_element_type=f32)


def by_eights(op, t):
    return op(t.reshape(t.shape[0] // 8, 8, t.shape[1]), axis=0)


def of_keys(head):
    at = head // REPEAT * HEAD
    return slice(at, at + HEAD)


def of_vals(head):
    at = WIDTH + head // REPEAT * HEAD
    return slice(at, at + HEAD)


def of_head(head):
    return slice(head * HEAD, (head + 1) * HEAD)


def self_bias(lens_ref, rows):
    key = lax.broadcasted_iota(jnp.int32, (rows, rows), 0)
    row = lax.broadcasted_iota(jnp.int32, (rows, rows), 1)
    key_seg = jnp.zeros((rows, rows), jnp.int32)
    row_seg = jnp.zeros((rows, rows), jnp.int32)
    end = jnp.int32(0)
    for i in range(lens_ref.shape[-1]):
        end = end + lens_ref[0, 0, i]
        key_seg += (key >= end).astype(jnp.int32)
        row_seg += (row >= end).astype(jnp.int32)
    return jnp.where((key_seg == row_seg) & (key <= row), 0.0, MASKED).astype(f32)


def scaled(t, factor):
    return (t.astype(f32) * factor).astype(bf16)


def of_group(head):
    at = head // REPEAT * HEAD
    return slice(at, at + HEAD)


def start_all(copies, semaphores):
    started = []
    for i, (source, target) in enumerate(copies):
        started.append(pltpu.make_async_copy(source, target, semaphores.at[i]))
        started[-1].start()
    return started


def wait_all(copies):
    for copy in copies:
        copy.wait()


def halves(ref):
    return ref.at[:, :WIDTH], ref.at[:, WIDTH:]


def eight(row):
    return jnp.broadcast_to(row, (8, row.shape[1]))


def places_of(chunks):
    return [slice(i * ROWS, (i + 1) * ROWS) for i in range(len(chunks))]


def forward(q_ref, chunks, bias_ref, low_ref, out_ref, stat_ref, scores_ref):
    places = places_of(chunks)
    vals_t = [[v[:, of_group(g * REPEAT)].T for _, v in chunks] for g in range(KV_HEADS)]
    tops = {}

    def score_pass(h):
        q_t = q_ref[0, :, of_head(h)].T
        top = None
        for at, (k, _) in zip(places, chunks):
            s = dot_nn(k[:, of_group(h)], q_t)
            if bias_ref is not None and at is places[-1]:
                s = s + bias_ref[...]
            scores_ref[h % 2, at] = s
            s = by_eights(jnp.max, s)
            top = s if top is None else jnp.maximum(top, s)
        tops[h] = jnp.max(top, axis=0, keepdims=True) * (SCALE * LOG2E)

    def weight_pass(h):
        sums, out_t = 0.0, 0.0
        for at, v_t in zip(places, vals_t[h // REPEAT]):
            weights = jnp.exp2(scores_ref[h % 2, at] * (SCALE * LOG2E) - tops[h])
            low = weights.astype(bf16)
            low_ref[h, at] = low
            sums = sums + by_eights(jnp.sum, weights)
            out_t = out_t + dot_nn(v_t, low)
        stat_ref[h, 0:8] = eight(tops[h])
        stat_ref[h, 8:16] = sums
        out_ref[h] = out_t.astype(bf16)

    score_pass(0)
    for h in range(HEADS):
        if h + 1 < HEADS:
            score_pass(h + 1)
        weight_pass(h)


def backward(q_ref, do_ref, chunks, lows, shares, stat_ref, acc, d_probs_ref, put_dq, put_sums):
    places = places_of(chunks)
    keys_t = [[k[:, of_group(g * REPEAT)].T for k, _ in chunks] for g in range(KV_HEADS)]
    d_outs = {}

    def d_probs_pass(h):
        d_outs[h] = do_ref[0, :, of_head(h)].T
        for at, (_, v) in zip(places, chunks):
            d_probs_ref[h % 2, at] = dot_nn(v[:, of_group(h)], d_outs[h])

    def add(h, j, at, new):
        acc[j, :, at] = new if h % REPEAT == 0 else acc[j, :, at] + new

    def gradient_pass(h):
        delta = stat_ref[h, 0:1]
        share = {at: stat_ref[h, at : at + 1] for at in set(shares)}
        do_scaled = {at: scaled(d_outs[h], t) for at, t in share.items()}
        q_t = q_ref[0, :, of_head(h)].T
        q_scaled = {at: scaled(q_t, t * SCALE) for at, t in share.items()}
        for at, low, which in zip(places, lows, shares):
            add(h, 1, at, dot_nt(do_scaled[which], low(h)))
        dq_t = {at: 0.0 for at in share}
        for at, low, which, k_t in zip(places, lows, shares, keys_t[h // REPEAT]):
            d_probs = d_probs_ref[h % 2, at] - delta
            d_scores = (low(h).astype(f32) * d_probs).astype(bf16)
            dq_t[which] = dq_t[which] + dot_nn(k_t, d_scores)
            add(h, 0, at, dot_nt(q_scaled[which], d_scores))
        put_dq(h, sum(dq_t[at] * (share[at] * SCALE) for at in sorted(share)))
        if h % REPEAT == REPEAT - 1:
            for j in range(2):
                put_sums(j, of_group(h), [acc[j, :, at].T for at in places])

    d_probs_pass(0)
    for h in range(HEADS):
        if h + 1 < HEADS:
            d_probs_pass(h + 1)
        gradient_pass(h)


def self_forward_kernel(
    lens_hbm, q_hbm, resp_hbm, low_hbm, out_hbm, stat_hbm,
    lens_ref, q_ref, resp_ref, bias_ref, scores_ref, low_ref, out_ref, stat_ref, arrived, left,
):
    arriving = start_all(((lens_hbm, lens_ref), (resp_hbm, resp_ref), (q_hbm, q_ref)), arrived)
    wait_all(arriving[:1])
    bias_ref[...] = self_bias(lens_ref, ROWS)
    wait_all(arriving[1:])
    chunks = [halves(resp_ref.at[0])]
    forward(q_ref, chunks, bias_ref, low_ref, out_ref, stat_ref, scores_ref)
    wait_all(start_all(((low_ref, low_hbm), (out_ref, out_hbm), (stat_ref, stat_hbm)), left))


def next_forward_kernel(
    q_ref, one_k, one_v, three_k, three_v, own_ref, low_ref, out_ref, stat_ref, scores_ref
):
    chunks = [(one_k, one_v), (three_k, three_v), halves(own_ref)]
    forward(q_ref, chunks, None, low_ref, out_ref, stat_ref, scores_ref)


def opposite_kernel(
    q_ref, do_ref, k_ref, v_ref, self_out_ref, self_stat_ref, next_out_ref, next_stat_ref,
    attn_ref, dq_ref, stat_ref, dk_ref, dv_ref, acc, scores_ref, low_ref, d_probs_ref,
):
    heads = range(0, HEADS, REPEAT)
    keys_t = [k_ref[:, of_group(h)].T for h in heads]
    vals_t = [v_ref[:, of_group(h)].T for h in heads]
    state = [{} for _ in range(HEADS)]

    def score_pass(h):
        q_t = q_ref[0, :, of_head(h)].T
        s = dot_nn(k_ref[:, of_group(h)], q_t)
        scores_ref[h % 2] = s
        top = by_eights(jnp.max, s) * (SCALE * LOG2E)
        top = jnp.maximum(jnp.maximum(self_stat_ref[h, 0:8], next_stat_ref[h, 0:8]), top)
        state[h].update(q_t=q_t, top=jnp.max(top, axis=0, keepdims=True))

    def weight_pass(h):
        top = state[h]["top"]
        weights = jnp.exp2(scores_ref[h % 2] * (SCALE * LOG2E) - top)
        low = weights.astype(bf16)
        low_ref[h % 4] = low
        own = jnp.exp2(self_stat_ref[h, 0:1] - top)
        next_ = jnp.exp2(next_stat_ref[h, 0:1] - top)
        sums = by_eights(jnp.sum, weights)
        sums = sums + self_stat_ref[h, 8:16] * own + next_stat_ref[h, 8:16] * next_
        inverse = 1.0 / jnp.sum(sums, axis=0, keepdims=True)
        out_t = self_out_ref[h].astype(f32) * own + next_out_ref[h].astype(f32) * next_
        out_t = (out_t + dot_nn(vals_t[h // REPEAT], low)) * inverse
        do_t = do_ref[0, :, of_head(h)].T
        d_probs_ref[h % 4] = dot_nn(v_ref[:, of_group(h)], do_t)
        stat_ref[h, 8:16] = eight(inverse * own)
        stat_ref[h, 16:24] = eight(inverse * next_)
        state[h].update(inverse=inverse, do_t=do_t, out_t=out_t)

    def delta_pass(h):
        do_t, out_t = state[h]["do_t"], state[h]["out_t"]
        delta = jnp.sum(
            do_t.astype(f32) * out_t.astype(bf16).astype(f32), axis=0, keepdims=True
        )
        stat_ref[h, 0:8] = eight(delta)
        attn_ref[0, :, of_head(h)] = out_t.T.astype(bf16)
        state[h]["delta"] = delta
        add(h, 1, dot_nt(scaled(do_t, state[h]["inverse"]), low_ref[h % 4]))

    def add(h, j, new):
        acc[j] = new if h % REPEAT == 0 else acc[j] + new

    def gradient_pass(h):
        inverse = state[h]["inverse"]
        d_probs = d_probs_ref[h % 4] - state[h]["delta"]
        d_scores = (low_ref[h % 4].astype(f32) * d_probs).astype(bf16)
        dq_ref[h] = dot_nn(keys_t[h // REPEAT], d_scores) * (inverse * SCALE)
        add(h, 0, dot_nt(scaled(state[h]["q_t"], inverse * SCALE), d_scores))
        if h % REPEAT == REPEAT - 1:
            dk_ref[:, of_group(h)] = acc[0].T.astype(bf16)
            dv_ref[:, of_group(h)] = acc[1].T.astype(bf16)

    passes = (gradient_pass, delta_pass, weight_pass, score_pass)
    for step in range(1 - len(passes), HEADS):
        for lag, one_pass in enumerate(passes):
            if 0 <= step + lag < HEADS:
                one_pass(step + lag)


def next_backward_kernel(
    q_ref, do_ref, one_k, one_v, three_k, three_v, low_ref, stat_ref, dq_part_ref,
    dq_ref, d_one_k, d_one_v, d_three_k, d_three_v, acc, d_probs_ref,
):
    def put_dq(h, dq_t):
        dq_ref[h] = dq_part_ref[h] + dq_t

    def put_sums(j, cols, sums):
        for t, ref in zip(sums, ((d_one_k, d_three_k), (d_one_v, d_three_v))[j]):
            ref[:, cols] = t.astype(ref.dtype)

    chunks = [(one_k, one_v), (three_k, three_v)]
    lows = [lambda h, at=at: low_ref[h, at] for at in places_of(chunks)]
    backward(q_ref, do_ref, chunks, lows, [16, 16], stat_ref, acc, d_probs_ref, put_dq, put_sums)


def near_backward_kernel(
    q_ref, do_ref, own_ref, resp_ref, low_ref, self_low_ref, stat_ref, dq_part_ref,
    dq_ref, d_own_ref, d_resp_ref, acc, d_probs_ref,
):
    def put_dq(h, dq_t):
        dq_ref[0, :, of_head(h)] = (dq_part_ref[h] + dq_t).T.astype(bf16)

    def put_sums(j, cols, sums):
        cols = slice(j * WIDTH + cols.start, j * WIDTH + cols.stop)
        d_own_ref[:, cols] = sums[0]
        d_resp_ref[0, :, cols] = sums[1].astype(bf16)

    chunks = [halves(own_ref), halves(resp_ref.at[0])]
    lows = [lambda h: low_ref[h], lambda h: self_low_ref[h]]
    backward(q_ref, do_ref, chunks, lows, [16, 8], stat_ref, acc, d_probs_ref, put_dq, put_sums)


def whole(shape):
    return pl.BlockSpec(shape, lambda i: (0,) * len(shape))


def call(kernel, name, outs, scratch, args, flops=ROWS, in_hbm=False, specs={}):
    hbm = pl.BlockSpec(memory_space=pltpu.HBM)
    if in_hbm:
        args = [pltpu.with_memory_space_constraint(t, pltpu.HBM) for t in args]
    return pl.pallas_call(
        kernel,
        grid=(1,),
        in_specs=[hbm if in_hbm else specs.get(i, whole(t.shape)) for i, t in enumerate(args)],
        out_specs=[hbm if in_hbm else whole(shape) for shape, _ in outs],
        out_shape=[
            pltpu.HBM(shape, dtype) if in_hbm else jax.ShapeDtypeStruct(shape, dtype)
            for shape, dtype in outs
        ],
        scratch_shapes=[pltpu.VMEM(*t) if isinstance(t, tuple) else t for t in scratch],
        compiler_params=pltpu.CompilerParams(vmem_limit_bytes=30 << 20),
        cost_estimate=pl.CostEstimate(flops=flops, bytes_accessed=ROWS, transcendentals=0),
        name=name,
    )(*args)


def added(*terms):
    return sum(t.astype(f32) for t in terms).astype(bf16)


def exchange(t, axes):
    return lax.all_to_all(t, axes, split_axis=0, concat_axis=0, tiled=True)


def to_neighbour(t, by):
    return lax.ppermute(t, "x", [(i, i ^ by) for i in range(lax.axis_size("x"))])


def on_device(q_resp, resp_kv, prompt_kv, d_out, resp_lengths):
    groups, own_rows, width = prompt_kv.shape
    ring = ("zl", "c", "zh", "y")
    copies = lax.axis_size(("zh", "y"))
    sent = jnp.broadcast_to(prompt_kv[:, None], (groups, copies, own_rows, width))
    own = exchange(sent.reshape(-1, own_rows, width), ring).reshape(-1, width)

    flat, resp_kind, prompt = (q_resp.shape, bf16), (resp_kv.shape, bf16), own.shape
    tall, stat_kind = (HEADS, HEAD, ROWS), ((HEADS, 16, ROWS), f32)
    parts = lambda n: [((HEADS, n * ROWS, ROWS), bf16), (tall, bf16), stat_kind]
    scores = lambda n: ((2, n * ROWS, ROWS), f32)
    sums = ((2, HEAD, 2 * ROWS), f32)
    self_low, self_out, self_stat = call(
        self_forward_kernel,
        "self_forward",
        parts(1),
        [
            pltpu.SMEM(resp_lengths.shape, jnp.int32),
            flat,
            resp_kind,
            ((ROWS, ROWS), f32),
            scores(1),
            *parts(1),
            pltpu.SemaphoreType.DMA((3,)),
            pltpu.SemaphoreType.DMA((3,)),
        ],
        [resp_lengths, q_resp, resp_kv],
        flops=1 << 33,
        in_hbm=True,
    )

    own, self_stat = lax.optimization_barrier((own, self_stat))
    own_k, own_v = own[:, :WIDTH], own[:, WIDTH:]
    one_k, three_v = to_neighbour(own_k, 1), to_neighbour(own_v, 3)
    one_v, three_k = to_neighbour(own_v, 1), to_neighbour(own_k, 3)
    far_k, far_v = to_neighbour(one_k, 3), to_neighbour(three_v, 1)
    next_ = [one_k, one_v, three_k, three_v]
    next_low, next_out, next_stat = call(
        next_forward_kernel, "next_forward", parts(3), [scores(3)], [q_resp, *next_, own]
    )
    half = lambda dtype: ((ROWS, WIDTH), dtype)
    attn, dq, stat, dk, dv = call(
        opposite_kernel,
        "opposite",
        [flat, (tall, f32), ((HEADS, 24, ROWS), f32), half(bf16), half(bf16)],
        [
            ((2, HEAD, ROWS), f32),
            ((2, ROWS, ROWS), f32),
            ((4, ROWS, ROWS), bf16),
            ((4, ROWS, ROWS), f32),
        ],
        [q_resp, d_out, far_k, far_v, self_out, self_stat, next_out, next_stat],
    )
    dk, dv = to_neighbour(dk, 3), to_neighbour(dv, 1)
    dq, d_one_k, d_one_v, d_three_k, d_three_v = call(
        next_backward_kernel,
        "next_backward",
        [(tall, f32), half(f32), half(bf16), half(bf16), half(f32)],
        [sums, scores(2)],
        [q_resp, d_out, *next_, next_low, stat, dq],
        specs={6: pl.BlockSpec((HEADS, 2 * ROWS, ROWS), lambda i: (0, 0, 0))},
    )
    d_one_v, d_three_k = to_neighbour(d_one_v, 1), to_neighbour(d_three_k, 3)
    dk, dv, d_one_k, d_three_v = lax.optimization_barrier((dk, dv, d_one_k, d_three_v))
    d_one_k, d_three_v = added(d_one_k, dk), added(d_three_v, dv)
    d_one_k, d_three_v = lax.optimization_barrier((d_one_k, d_three_v))
    d_one_k, d_three_v = to_neighbour(d_one_k, 1), to_neighbour(d_three_v, 3)
    dq, d_own, d_resp = call(
        near_backward_kernel,
        "near_backward",
        [flat, (prompt, f32), resp_kind],
        [sums, scores(2)],
        [q_resp, d_out, own, resp_kv, next_low, self_low, stat, dq],
        specs={4: pl.BlockSpec((HEADS, ROWS, ROWS), lambda i: (0, 2, 0))},
    )
    came = (d_one_k, d_three_k, d_one_v, d_three_v)
    d_own, *came = lax.optimization_barrier((d_own, *came))
    keys = added(d_own[:, :WIDTH], came[0], came[1])
    vals = added(d_own[:, WIDTH:], came[2], came[3])
    total = jnp.concatenate([keys, vals], 1)
    total = exchange(total.reshape(-1, own_rows, width), ring)
    total = total.reshape(groups, copies, own_rows, width)
    d_prompt = jnp.sum(total.astype(f32), axis=1).astype(bf16)
    return attn, dq, d_resp, d_prompt


def solution(mesh):
    fine = Mesh(mesh.devices.reshape(4, 2, 2, 4, 4), ("zl", "c", "zh", "y", "x"))
    grp, seq = ("zl", "c"), ("zh", "y", "x")
    rows = P(grp, seq, None)
    prompt = P(None, grp + seq, None)
    return jax.shard_map(
        on_device,
        mesh=fine,
        in_specs=(rows, rows, prompt, rows, rows),
        out_specs=(rows, rows, rows, prompt),
        check_vma=False,
    )
```

```python
import functools

import jax
import jax.numpy as jnp
from jax import lax
from jax.experimental import pallas as pl
from jax.experimental.pallas import tpu as pltpu
from jax.sharding import Mesh
from jax.sharding import PartitionSpec as P

HEADS = 10
KV_HEADS = 2
HEAD = 128
REPEAT = HEADS // KV_HEADS
SCALE = HEAD ** (-0.5)
LOG2E = 1.4426950408889634
MASKED = -1e30
WIDTH = KV_HEADS * HEAD
ROWS = 256
bf16 = jnp.bfloat16
f32 = jnp.float32


def dot_nn(a, b):
    return lax.dot_general(a, b, (((1,), (0,)), ((), ())), preferred_element_type=f32)


def dot_nt(a, b):
    return lax.dot_general(a, b, (((1,), (1,)), ((), ())), preferred_element_type=f32)


def by_eights(op, t):
    return op(t.reshape(t.shape[0] // 8, 8, t.shape[1]), axis=0)


def of_keys(head):
    at = head // REPEAT * HEAD
    return slice(at, at + HEAD)


def of_vals(head):
    at = WIDTH + head // REPEAT * HEAD
    return slice(at, at + HEAD)


def of_head(head):
    return slice(head * HEAD, (head + 1) * HEAD)


def self_bias(lens_ref, rows):
    key = lax.broadcasted_iota(jnp.int32, (rows, rows), 0)
    row = lax.broadcasted_iota(jnp.int32, (rows, rows), 1)
    key_seg = jnp.zeros((rows, rows), jnp.int32)
    row_seg = jnp.zeros((rows, rows), jnp.int32)
    end = jnp.int32(0)
    for i in range(lens_ref.shape[-1]):
        end = end + lens_ref[0, 0, i]
        key_seg += (key >= end).astype(jnp.int32)
        row_seg += (row >= end).astype(jnp.int32)
    return jnp.where((key_seg == row_seg) & (key <= row), 0.0, MASKED).astype(f32)


def scaled(t, factor):
    return (t.astype(f32) * factor).astype(bf16)


def of_group(head):
    at = head // REPEAT * HEAD
    return slice(at, at + HEAD)


def start_all(copies, semaphores):
    started = []
    for i, (source, target) in enumerate(copies):
        started.append(pltpu.make_async_copy(source, target, semaphores.at[i]))
        started[-1].start()
    return started


def wait_all(copies):
    for copy in copies:
        copy.wait()


def halves(ref):
    return ref.at[:, :WIDTH], ref.at[:, WIDTH:]


def eight(row):
    return jnp.broadcast_to(row, (8, row.shape[1]))


def places_of(chunks):
    return [slice(i * ROWS, (i + 1) * ROWS) for i in range(len(chunks))]


def forward(q_ref, chunks, bias_ref, low_ref, out_ref, stat_ref, scores_ref):
    places = places_of(chunks)
    vals_t = [[v[:, of_group(g * REPEAT)].T for _, v in chunks] for g in range(KV_HEADS)]
    tops = {}

    def score_pass(h):
        q_t = q_ref[0, :, of_head(h)].T
        top = None
        for at, (k, _) in zip(places, chunks):
            s = dot_nn(k[:, of_group(h)], q_t)
            if bias_ref is not None and at is places[-1]:
                s = s + bias_ref[...]
            scores_ref[h % 2, at] = s
            s = by_eights(jnp.max, s)
            top = s if top is None else jnp.maximum(top, s)
        tops[h] = jnp.max(top, axis=0, keepdims=True) * (SCALE * LOG2E)

    def weight_pass(h):
        sums, out_t = 0.0, 0.0
        for at, v_t in zip(places, vals_t[h // REPEAT]):
            weights = jnp.exp2(scores_ref[h % 2, at] * (SCALE * LOG2E) - tops[h])
            low = weights.astype(bf16)
            low_ref[h, at] = low
            sums = sums + by_eights(jnp.sum, weights)
            out_t = out_t + dot_nn(v_t, low)
        stat_ref[h, 0:8] = eight(tops[h])
        stat_ref[h, 8:16] = sums
        out_ref[h] = out_t.astype(bf16)

    score_pass(0)
    for h in range(HEADS):
        if h + 1 < HEADS:
            score_pass(h + 1)
        weight_pass(h)


def backward(q_ref, do_ref, chunks, lows, shares, stat_ref, acc, d_probs_ref, put_dq, put_sums):
    places = places_of(chunks)
    keys_t = [[k[:, of_group(g * REPEAT)].T for k, _ in chunks] for g in range(KV_HEADS)]
    d_outs = {}

    def d_probs_pass(h):
        d_outs[h] = do_ref[0, :, of_head(h)].T
        for at, (_, v) in zip(places, chunks):
            d_probs_ref[h % 2, at] = dot_nn(v[:, of_group(h)], d_outs[h])

    def add(h, j, at, new):
        acc[j, :, at] = new if h % REPEAT == 0 else acc[j, :, at] + new

    def gradient_pass(h):
        delta = stat_ref[h, 0:1]
        share = {at: stat_ref[h, at : at + 1] for at in set(shares)}
        do_scaled = {at: scaled(d_outs[h], t) for at, t in share.items()}
        q_t = q_ref[0, :, of_head(h)].T
        q_scaled = {at: scaled(q_t, t * SCALE) for at, t in share.items()}
        for at, low, which in zip(places, lows, shares):
            add(h, 1, at, dot_nt(do_scaled[which], low(h)))
        dq_t = {at: 0.0 for at in share}
        for at, low, which, k_t in zip(places, lows, shares, keys_t[h // REPEAT]):
            d_probs = d_probs_ref[h % 2, at] - delta
            d_scores = (low(h).astype(f32) * d_probs).astype(bf16)
            dq_t[which] = dq_t[which] + dot_nn(k_t, d_scores)
            add(h, 0, at, dot_nt(q_scaled[which], d_scores))
        put_dq(h, sum(dq_t[at] * (share[at] * SCALE) for at in sorted(share)))
        if h % REPEAT == REPEAT - 1:
            for j in range(2):
                put_sums(j, of_group(h), [acc[j, :, at].T for at in places])

    d_probs_pass(0)
    for h in range(HEADS):
        if h + 1 < HEADS:
            d_probs_pass(h + 1)
        gradient_pass(h)


def self_forward_kernel(
    lens_hbm, q_hbm, resp_hbm, low_hbm, out_hbm, stat_hbm,
    lens_ref, q_ref, resp_ref, bias_ref, scores_ref, low_ref, out_ref, stat_ref, arrived, left,
):
    arriving = start_all(((lens_hbm, lens_ref), (resp_hbm, resp_ref), (q_hbm, q_ref)), arrived)
    wait_all(arriving[:1])
    bias_ref[...] = self_bias(lens_ref, ROWS)
    wait_all(arriving[1:])
    chunks = [halves(resp_ref.at[0])]
    forward(q_ref, chunks, bias_ref, low_ref, out_ref, stat_ref, scores_ref)
    wait_all(start_all(((low_ref, low_hbm), (out_ref, out_hbm), (stat_ref, stat_hbm)), left))


def next_forward_kernel(
    q_ref, one_k, one_v, three_k, three_v, own_ref, low_ref, out_ref, stat_ref, scores_ref
):
    chunks = [(one_k, one_v), (three_k, three_v), halves(own_ref)]
    forward(q_ref, chunks, None, low_ref, out_ref, stat_ref, scores_ref)


def opposite_kernel(
    q_ref, do_ref, k_ref, v_ref, self_out_ref, self_stat_ref, next_out_ref, next_stat_ref,
    out_ref, dq_ref, stat_ref, dk_ref, dv_ref, acc, scores_ref, low_ref, d_probs_ref,
):
    heads = range(0, HEADS, REPEAT)
    keys_t = [k_ref[:, of_group(h)].T for h in heads]
    vals_t = [v_ref[:, of_group(h)].T for h in heads]
    state = [{} for _ in range(HEADS)]

    def score_pass(h):
        q_t = q_ref[0, :, of_head(h)].T
        s = dot_nn(k_ref[:, of_group(h)], q_t)
        scores_ref[h % 2] = s
        top = by_eights(jnp.max, s) * (SCALE * LOG2E)
        top = jnp.maximum(jnp.maximum(self_stat_ref[h, 0:8], next_stat_ref[h, 0:8]), top)
        state[h].update(q_t=q_t, top=jnp.max(top, axis=0, keepdims=True))

    def weight_pass(h):
        top = state[h]["top"]
        weights = jnp.exp2(scores_ref[h % 2] * (SCALE * LOG2E) - top)
        low = weights.astype(bf16)
        low_ref[h % 4] = low
        own = jnp.exp2(self_stat_ref[h, 0:1] - top)
        next_ = jnp.exp2(next_stat_ref[h, 0:1] - top)
        sums = by_eights(jnp.sum, weights)
        sums = sums + self_stat_ref[h, 8:16] * own + next_stat_ref[h, 8:16] * next_
        inverse = 1.0 / jnp.sum(sums, axis=0, keepdims=True)
        out_t = self_out_ref[h].astype(f32) * own + next_out_ref[h].astype(f32) * next_
        out_t = (out_t + dot_nn(vals_t[h // REPEAT], low)) * inverse
        do_t = do_ref[0, :, of_head(h)].T
        d_probs_ref[h % 4] = dot_nn(v_ref[:, of_group(h)], do_t)
        stat_ref[h, 8:16] = eight(inverse * own)
        stat_ref[h, 16:24] = eight(inverse * next_)
        state[h].update(inverse=inverse, do_t=do_t, out_t=out_t)

    def delta_pass(h):
        do_t, out_t = state[h]["do_t"], state[h]["out_t"]
        delta = jnp.sum(
            do_t.astype(f32) * out_t.astype(bf16).astype(f32), axis=0, keepdims=True
        )
        stat_ref[h, 0:8] = eight(delta)
        out_ref[h] = out_t.astype(bf16)
        state[h]["delta"] = delta
        add(h, 1, dot_nt(scaled(do_t, state[h]["inverse"]), low_ref[h % 4]))

    def add(h, j, new):
        at = (h // REPEAT, j)
        acc[at] = new if h % REPEAT == 0 else acc[at] + new

    def gradient_pass(h):
        inverse = state[h]["inverse"]
        d_probs = d_probs_ref[h % 4] - state[h]["delta"]
        d_scores = (low_ref[h % 4].astype(f32) * d_probs).astype(bf16)
        dq_ref[h] = dot_nn(keys_t[h // REPEAT], d_scores) * (inverse * SCALE)
        add(h, 0, dot_nt(scaled(state[h]["q_t"], inverse * SCALE), d_scores))
        if h % REPEAT == REPEAT - 1:
            dk_ref[:, of_group(h)] = acc[h // REPEAT, 0].T.astype(bf16)
            dv_ref[:, of_group(h)] = acc[h // REPEAT, 1].T.astype(bf16)

    passes = (gradient_pass, delta_pass, weight_pass, score_pass)
    for step in range(1 - len(passes), HEADS):
        for lag in (1, 3, 0, 2):
            if 0 <= step + lag < HEADS:
                passes[lag](step + lag)


def next_backward_kernel(
    q_ref, do_ref, one_k, one_v, three_k, three_v, low_ref, stat_ref, dq_part_ref,
    dq_ref, d_one_k, d_one_v, d_three_k, d_three_v, acc, d_probs_ref,
):
    def put_dq(h, dq_t):
        dq_ref[h] = dq_part_ref[h] + dq_t

    def put_sums(j, cols, sums):
        for t, ref in zip(sums, ((d_one_k, d_three_k), (d_one_v, d_three_v))[j]):
            ref[:, cols] = t.astype(ref.dtype)

    chunks = [(one_k, one_v), (three_k, three_v)]
    lows = [lambda h, at=at: low_ref[h, at] for at in places_of(chunks)]
    backward(q_ref, do_ref, chunks, lows, [16, 16], stat_ref, acc, d_probs_ref, put_dq, put_sums)


def near_backward_kernel(
    q_ref, do_ref, own_ref, resp_ref, low_ref, self_low_ref, stat_ref, dq_part_ref, out_ref,
    attn_ref, dq_ref, d_own_ref, d_resp_ref, acc, d_probs_ref,
):
    def put_dq(h, dq_t):
        dq_ref[0, :, of_head(h)] = (dq_part_ref[h] + dq_t).T.astype(bf16)
        attn_ref[0, :, of_head(h)] = out_ref[h].T

    def put_sums(j, cols, sums):
        cols = slice(j * WIDTH + cols.start, j * WIDTH + cols.stop)
        d_own_ref[:, cols] = sums[0]
        d_resp_ref[0, :, cols] = sums[1].astype(bf16)

    chunks = [halves(own_ref), halves(resp_ref.at[0])]
    lows = [lambda h: low_ref[h], lambda h: self_low_ref[h]]
    backward(q_ref, do_ref, chunks, lows, [16, 8], stat_ref, acc, d_probs_ref, put_dq, put_sums)


def whole(shape):
    return pl.BlockSpec(shape, lambda i: (0,) * len(shape))


def call(kernel, name, outs, scratch, args, flops=ROWS, in_hbm=False, specs={}):
    hbm = pl.BlockSpec(memory_space=pltpu.HBM)
    if in_hbm:
        args = [pltpu.with_memory_space_constraint(t, pltpu.HBM) for t in args]
    return pl.pallas_call(
        kernel,
        grid=(1,),
        in_specs=[hbm if in_hbm else specs.get(i, whole(t.shape)) for i, t in enumerate(args)],
        out_specs=[hbm if in_hbm else whole(shape) for shape, _ in outs],
        out_shape=[
            pltpu.HBM(shape, dtype) if in_hbm else jax.ShapeDtypeStruct(shape, dtype)
            for shape, dtype in outs
        ],
        scratch_shapes=[pltpu.VMEM(*t) if isinstance(t, tuple) else t for t in scratch],
        compiler_params=pltpu.CompilerParams(vmem_limit_bytes=30 << 20),
        cost_estimate=pl.CostEstimate(flops=flops, bytes_accessed=ROWS, transcendentals=0),
        name=name,
    )(*args)


def added(*terms):
    return sum(t.astype(f32) for t in terms).astype(bf16)


def exchange(t, axes):
    return lax.all_to_all(t, axes, split_axis=0, concat_axis=0, tiled=True)


def to_neighbour(t, side):
    size = lax.axis_size("x")
    by = ((1, 3), (3, 1))
    pairs = [
        (core * size + i, core * size + (i ^ by[core][side]))
        for core in range(lax.axis_size("c"))
        for i in range(size)
    ]
    return lax.ppermute(t, ("c", "x"), pairs)


def on_device(q_resp, resp_kv, prompt_kv, d_out, resp_lengths):
    groups, own_rows, width = prompt_kv.shape
    ring = ("zl", "c", "zh", "y")
    copies = lax.axis_size(("zh", "y"))
    sent = jnp.broadcast_to(prompt_kv[:, None], (groups, copies, own_rows, width))
    own = exchange(sent.reshape(-1, own_rows, width), ring).reshape(-1, width)

    flat, resp_kind, prompt = (q_resp.shape, bf16), (resp_kv.shape, bf16), own.shape
    tall, stat_kind = (HEADS, HEAD, ROWS), ((HEADS, 16, ROWS), f32)
    parts = lambda n: [((HEADS, n * ROWS, ROWS), bf16), (tall, bf16), stat_kind]
    scores = lambda n: ((2, n * ROWS, ROWS), f32)
    sums = ((2, HEAD, 2 * ROWS), f32)
    self_low, self_out, self_stat = call(
        self_forward_kernel,
        "self_forward",
        parts(1),
        [
            pltpu.SMEM(resp_lengths.shape, jnp.int32),
            flat,
            resp_kind,
            ((ROWS, ROWS), f32),
            scores(1),
            *parts(1),
            pltpu.SemaphoreType.DMA((3,)),
            pltpu.SemaphoreType.DMA((3,)),
        ],
        [resp_lengths, q_resp, resp_kv],
        flops=1 << 33,
        in_hbm=True,
    )

    own, self_stat = lax.optimization_barrier((own, self_stat))
    own_k, own_v = own[:, :WIDTH], own[:, WIDTH:]
    one_k, three_v = to_neighbour(own_k, 0), to_neighbour(own_v, 1)
    one_v, three_k = to_neighbour(own_v, 0), to_neighbour(own_k, 1)
    far_k, far_v = to_neighbour(one_k, 1), to_neighbour(three_v, 0)
    next_ = [one_k, one_v, three_k, three_v]
    next_low, next_out, next_stat = call(
        next_forward_kernel, "next_forward", parts(3), [scores(3)], [q_resp, *next_, own]
    )
    half = lambda dtype: ((ROWS, WIDTH), dtype)
    out, dq, stat, dk, dv = call(
        opposite_kernel,
        "opposite",
        [(tall, bf16), (tall, f32), ((HEADS, 24, ROWS), f32), half(bf16), half(bf16)],
        [
            ((KV_HEADS, 2, HEAD, ROWS), f32),
            ((2, ROWS, ROWS), f32),
            ((4, ROWS, ROWS), bf16),
            ((4, ROWS, ROWS), f32),
        ],
        [q_resp, d_out, far_k, far_v, self_out, self_stat, next_out, next_stat],
    )
    dk, dv = to_neighbour(dk, 1), to_neighbour(dv, 0)
    dq, d_one_k, d_one_v, d_three_k, d_three_v = call(
        next_backward_kernel,
        "next_backward",
        [(tall, f32), half(f32), half(bf16), half(bf16), half(f32)],
        [sums, scores(2)],
        [q_resp, d_out, *next_, next_low, stat, dq],
        specs={6: pl.BlockSpec((HEADS, 2 * ROWS, ROWS), lambda i: (0, 0, 0))},
    )
    d_one_v, d_three_k = to_neighbour(d_one_v, 0), to_neighbour(d_three_k, 1)
    dk, dv, d_one_k, d_three_v = lax.optimization_barrier((dk, dv, d_one_k, d_three_v))
    d_one_k, d_three_v = added(d_one_k, dk), added(d_three_v, dv)
    d_one_k, d_three_v = lax.optimization_barrier((d_one_k, d_three_v))
    d_one_k, d_three_v = to_neighbour(d_one_k, 0), to_neighbour(d_three_v, 1)
    attn, dq, d_own, d_resp = call(
        near_backward_kernel,
        "near_backward",
        [flat, flat, (prompt, f32), resp_kind],
        [sums, scores(2)],
        [q_resp, d_out, own, resp_kv, next_low, self_low, stat, dq, out],
        specs={4: pl.BlockSpec((HEADS, ROWS, ROWS), lambda i: (0, 2, 0))},
    )
    came = (d_one_k, d_three_k, d_one_v, d_three_v)
    d_own, *came = lax.optimization_barrier((d_own, *came))
    keys = added(d_own[:, :WIDTH], came[0], came[1])
    vals = added(d_own[:, WIDTH:], came[2], came[3])
    total = jnp.concatenate([keys, vals], 1)
    total = exchange(total.reshape(-1, own_rows, width), ring)
    total = total.reshape(groups, copies, own_rows, width)
    d_prompt = jnp.sum(total.astype(f32), axis=1).astype(bf16)
    return attn, dq, d_resp, d_prompt


def solution(mesh):
    fine = Mesh(mesh.devices.reshape(4, 2, 2, 4, 4), ("zl", "c", "zh", "y", "x"))
    grp, seq = ("zl", "c"), ("zh", "y", "x")
    rows = P(grp, seq, None)
    prompt = P(None, grp + seq, None)
    return jax.shard_map(
        on_device,
        mesh=fine,
        in_specs=(rows, rows, prompt, rows, rows),
        out_specs=(rows, rows, rows, prompt),
        check_vma=False,
    )
```

```python
import functools

import jax
import jax.numpy as jnp
from jax import lax
from jax.experimental import pallas as pl
from jax.experimental.pallas import tpu as pltpu
from jax.sharding import Mesh
from jax.sharding import PartitionSpec as P

HEADS = 10
KV_HEADS = 2
HEAD = 128
REPEAT = HEADS // KV_HEADS
SCALE = HEAD ** (-0.5)
LOG2E = 1.4426950408889634
MASKED = -1e30
WIDTH = KV_HEADS * HEAD
ROWS = 256
bf16 = jnp.bfloat16
f32 = jnp.float32


def dot_nn(a, b):
    return lax.dot_general(a, b, (((1,), (0,)), ((), ())), preferred_element_type=f32)


def dot_nt(a, b):
    return lax.dot_general(a, b, (((1,), (1,)), ((), ())), preferred_element_type=f32)


def by_eights(op, t):
    return op(t.reshape(t.shape[0] // 8, 8, t.shape[1]), axis=0)


def of_keys(head):
    at = head // REPEAT * HEAD
    return slice(at, at + HEAD)


def of_vals(head):
    at = WIDTH + head // REPEAT * HEAD
    return slice(at, at + HEAD)


def of_head(head):
    return slice(head * HEAD, (head + 1) * HEAD)


def self_bias(lens_ref, rows):
    key = lax.broadcasted_iota(jnp.int32, (rows, rows), 0)
    row = lax.broadcasted_iota(jnp.int32, (rows, rows), 1)
    key_seg = jnp.zeros((rows, rows), jnp.int32)
    row_seg = jnp.zeros((rows, rows), jnp.int32)
    end = jnp.int32(0)
    for i in range(lens_ref.shape[-1]):
        end = end + lens_ref[0, 0, i]
        key_seg += (key >= end).astype(jnp.int32)
        row_seg += (row >= end).astype(jnp.int32)
    return jnp.where((key_seg == row_seg) & (key <= row), 0.0, MASKED).astype(f32)


def scaled(t, factor):
    return (t.astype(f32) * factor).astype(bf16)


def of_group(head):
    at = head // REPEAT * HEAD
    return slice(at, at + HEAD)


def start_all(copies, semaphores):
    started = []
    for i, (source, target) in enumerate(copies):
        started.append(pltpu.make_async_copy(source, target, semaphores.at[i]))
        started[-1].start()
    return started


def wait_all(copies):
    for copy in copies:
        copy.wait()


def halves(ref):
    return ref.at[:, :WIDTH], ref.at[:, WIDTH:]


def eight(row):
    return jnp.broadcast_to(row, (8, row.shape[1]))


def places_of(chunks):
    return [slice(i * ROWS, (i + 1) * ROWS) for i in range(len(chunks))]


def forward(q_ref, chunks, bias_ref, low_ref, out_ref, stat_ref, scores_ref):
    places = places_of(chunks)
    vals_t = [[v[:, of_group(g * REPEAT)].T for _, v in chunks] for g in range(KV_HEADS)]
    tops = {}

    def score_pass(h):
        q_t = q_ref[0, :, of_head(h)].T
        top = None
        for at, (k, _) in zip(places, chunks):
            s = dot_nn(k[:, of_group(h)], q_t)
            if bias_ref is not None and at is places[-1]:
                s = s + bias_ref[...]
            scores_ref[h % 3, at] = s
            s = by_eights(jnp.max, s)
            top = s if top is None else jnp.maximum(top, s)
        tops[h] = jnp.max(top, axis=0, keepdims=True) * (SCALE * LOG2E)

    def weight_pass(h):
        sums, out_t = 0.0, 0.0
        for at, v_t in zip(places, vals_t[h // REPEAT]):
            weights = jnp.exp2(scores_ref[h % 3, at] * (SCALE * LOG2E) - tops[h])
            low = weights.astype(bf16)
            low_ref[h, at] = low
            sums = sums + by_eights(jnp.sum, weights)
            out_t = out_t + dot_nn(v_t, low)
        stat_ref[h, 0:8] = eight(tops[h])
        stat_ref[h, 8:16] = sums
        out_ref[h] = out_t.astype(bf16)

    score_pass(0)
    score_pass(1)
    for h in range(HEADS):
        weight_pass(h)
        if h + 2 < HEADS:
            score_pass(h + 2)


def backward(q_ref, do_ref, chunks, lows, shares, stat_ref, acc, d_probs_ref, put_dq, put_sums):
    places = places_of(chunks)
    keys_t = [[k[:, of_group(g * REPEAT)].T for k, _ in chunks] for g in range(KV_HEADS)]
    d_outs = {}

    def d_probs_pass(h):
        d_outs[h] = do_ref[0, :, of_head(h)].T
        for at, (_, v) in zip(places, chunks):
            d_probs_ref[h % 3, at] = dot_nn(v[:, of_group(h)], d_outs[h])

    def add(h, j, at, new):
        acc[j, :, at] = new if h % REPEAT == 0 else acc[j, :, at] + new

    def gradient_pass(h):
        delta = stat_ref[h, 0:1]
        share = {at: stat_ref[h, at : at + 1] for at in set(shares)}
        do_scaled = {at: scaled(d_outs[h], t) for at, t in share.items()}
        q_t = q_ref[0, :, of_head(h)].T
        q_scaled = {at: scaled(q_t, t * SCALE) for at, t in share.items()}
        for at, low, which in zip(places, lows, shares):
            add(h, 1, at, dot_nt(do_scaled[which], low(h)))
        dq_t = {at: 0.0 for at in share}
        for at, low, which, k_t in zip(places, lows, shares, keys_t[h // REPEAT]):
            d_probs = d_probs_ref[h % 3, at] - delta
            d_scores = (low(h).astype(f32) * d_probs).astype(bf16)
            dq_t[which] = dq_t[which] + dot_nn(k_t, d_scores)
            add(h, 0, at, dot_nt(q_scaled[which], d_scores))
        put_dq(h, sum(dq_t[at] * (share[at] * SCALE) for at in sorted(share)))
        if h % REPEAT == REPEAT - 1:
            for j in range(2):
                put_sums(j, of_group(h), [acc[j, :, at].T for at in places])

    d_probs_pass(0)
    d_probs_pass(1)
    for h in range(HEADS):
        gradient_pass(h)
        if h + 2 < HEADS:
            d_probs_pass(h + 2)


def self_forward_kernel(
    lens_hbm, q_hbm, resp_hbm, low_hbm, out_hbm, stat_hbm,
    lens_ref, q_ref, resp_ref, bias_ref, scores_ref, low_ref, out_ref, stat_ref, arrived, left,
):
    arriving = start_all(((lens_hbm, lens_ref), (resp_hbm, resp_ref), (q_hbm, q_ref)), arrived)
    wait_all(arriving[:1])
    bias_ref[...] = self_bias(lens_ref, ROWS)
    wait_all(arriving[1:])
    chunks = [halves(resp_ref.at[0])]
    forward(q_ref, chunks, bias_ref, low_ref, out_ref, stat_ref, scores_ref)
    wait_all(start_all(((low_ref, low_hbm), (out_ref, out_hbm), (stat_ref, stat_hbm)), left))


def next_forward_kernel(
    q_ref, one_k, one_v, three_k, three_v, own_ref, low_ref, out_ref, stat_ref, scores_ref
):
    chunks = [(one_k, one_v), (three_k, three_v), halves(own_ref)]
    forward(q_ref, chunks, None, low_ref, out_ref, stat_ref, scores_ref)


def opposite_kernel(
    q_ref, do_ref, k_ref, v_ref, self_out_ref, self_stat_ref, next_out_ref, next_stat_ref,
    out_ref, dq_ref, stat_ref, dk_ref, dv_ref, acc, scores_ref, low_ref, d_probs_ref,
):
    heads = range(0, HEADS, REPEAT)
    keys_t = [k_ref[:, of_group(h)].T for h in heads]
    vals_t = [v_ref[:, of_group(h)].T for h in heads]
    state = [{} for _ in range(HEADS)]

    def score_pass(h):
        q_t = q_ref[0, :, of_head(h)].T
        s = dot_nn(k_ref[:, of_group(h)], q_t)
        scores_ref[h % 2] = s
        top = by_eights(jnp.max, s) * (SCALE * LOG2E)
        top = jnp.maximum(jnp.maximum(self_stat_ref[h, 0:8], next_stat_ref[h, 0:8]), top)
        state[h].update(q_t=q_t, top=jnp.max(top, axis=0, keepdims=True))

    def weight_pass(h):
        top = state[h]["top"]
        weights = jnp.exp2(scores_ref[h % 2] * (SCALE * LOG2E) - top)
        low = weights.astype(bf16)
        low_ref[h % 4] = low
        own = jnp.exp2(self_stat_ref[h, 0:1] - top)
        next_ = jnp.exp2(next_stat_ref[h, 0:1] - top)
        sums = by_eights(jnp.sum, weights)
        sums = sums + self_stat_ref[h, 8:16] * own + next_stat_ref[h, 8:16] * next_
        inverse = 1.0 / jnp.sum(sums, axis=0, keepdims=True)
        out_t = self_out_ref[h].astype(f32) * own + next_out_ref[h].astype(f32) * next_
        out_t = (out_t + dot_nn(vals_t[h // REPEAT], low)) * inverse
        do_t = do_ref[0, :, of_head(h)].T
        d_probs_ref[h % 4] = dot_nn(v_ref[:, of_group(h)], do_t)
        stat_ref[h, 8:16] = eight(inverse * own)
        stat_ref[h, 16:24] = eight(inverse * next_)
        state[h].update(inverse=inverse, do_t=do_t, out_t=out_t)

    def delta_pass(h):
        do_t, out_t = state[h]["do_t"], state[h]["out_t"]
        delta = jnp.sum(
            do_t.astype(f32) * out_t.astype(bf16).astype(f32), axis=0, keepdims=True
        )
        stat_ref[h, 0:8] = eight(delta)
        out_ref[h] = out_t.astype(bf16)
        state[h]["delta"] = delta
        add(h, 1, dot_nt(scaled(do_t, state[h]["inverse"]), low_ref[h % 4]))

    def add(h, j, new):
        at = (h // REPEAT, j)
        acc[at] = new if h % REPEAT == 0 else acc[at] + new

    def gradient_pass(h):
        inverse = state[h]["inverse"]
        d_probs = d_probs_ref[h % 4] - state[h]["delta"]
        d_scores = (low_ref[h % 4].astype(f32) * d_probs).astype(bf16)
        dq_ref[h] = dot_nn(keys_t[h // REPEAT], d_scores) * (inverse * SCALE)
        add(h, 0, dot_nt(scaled(state[h]["q_t"], inverse * SCALE), d_scores))
        if h % REPEAT == REPEAT - 1:
            dk_ref[:, of_group(h)] = acc[h // REPEAT, 0].T.astype(bf16)
            dv_ref[:, of_group(h)] = acc[h // REPEAT, 1].T.astype(bf16)

    passes = (gradient_pass, delta_pass, weight_pass, score_pass)
    for step in range(1 - len(passes), HEADS):
        for lag in (1, 3, 0, 2):
            if 0 <= step + lag < HEADS:
                passes[lag](step + lag)


def next_backward_kernel(
    q_ref, do_ref, one_k, one_v, three_k, three_v, low_ref, stat_ref, dq_part_ref,
    dq_ref, d_one_k, d_one_v, d_three_k, d_three_v, acc, d_probs_ref,
):
    def put_dq(h, dq_t):
        dq_ref[h] = dq_part_ref[h] + dq_t

    def put_sums(j, cols, sums):
        for t, ref in zip(sums, ((d_one_k, d_three_k), (d_one_v, d_three_v))[j]):
            ref[:, cols] = t.astype(ref.dtype)

    chunks = [(one_k, one_v), (three_k, three_v)]
    lows = [lambda h, at=at: low_ref[h, at] for at in places_of(chunks)]
    backward(q_ref, do_ref, chunks, lows, [16, 16], stat_ref, acc, d_probs_ref, put_dq, put_sums)


def near_backward_kernel(
    q_ref, do_ref, own_ref, resp_ref, low_ref, self_low_ref, stat_ref, dq_part_ref, out_ref,
    attn_ref, dq_ref, d_own_ref, d_resp_ref, acc, d_probs_ref,
):
    def put_dq(h, dq_t):
        dq_ref[0, :, of_head(h)] = (dq_part_ref[h] + dq_t).T.astype(bf16)
        attn_ref[0, :, of_head(h)] = out_ref[h].T

    def put_sums(j, cols, sums):
        cols = slice(j * WIDTH + cols.start, j * WIDTH + cols.stop)
        d_own_ref[:, cols] = sums[0]
        d_resp_ref[0, :, cols] = sums[1].astype(bf16)

    chunks = [halves(own_ref), halves(resp_ref.at[0])]
    lows = [lambda h: low_ref[h], lambda h: self_low_ref[h]]
    backward(q_ref, do_ref, chunks, lows, [16, 8], stat_ref, acc, d_probs_ref, put_dq, put_sums)


def whole(shape):
    return pl.BlockSpec(shape, lambda i: (0,) * len(shape))


def call(kernel, name, outs, scratch, args, flops=ROWS, in_hbm=False, specs={}):
    hbm = pl.BlockSpec(memory_space=pltpu.HBM)
    if in_hbm:
        args = [pltpu.with_memory_space_constraint(t, pltpu.HBM) for t in args]
    return pl.pallas_call(
        kernel,
        grid=(1,),
        in_specs=[hbm if in_hbm else specs.get(i, whole(t.shape)) for i, t in enumerate(args)],
        out_specs=[hbm if in_hbm else whole(shape) for shape, _ in outs],
        out_shape=[
            pltpu.HBM(shape, dtype) if in_hbm else jax.ShapeDtypeStruct(shape, dtype)
            for shape, dtype in outs
        ],
        scratch_shapes=[pltpu.VMEM(*t) if isinstance(t, tuple) else t for t in scratch],
        compiler_params=pltpu.CompilerParams(vmem_limit_bytes=30 << 20),
        cost_estimate=pl.CostEstimate(flops=flops, bytes_accessed=ROWS, transcendentals=0),
        name=name,
    )(*args)


def added(*terms):
    return sum(t.astype(f32) for t in terms).astype(bf16)


def exchange(t, axes):
    return lax.all_to_all(t, axes, split_axis=0, concat_axis=0, tiled=True)


def to_neighbour(t, side):
    size = lax.axis_size("x")
    by = ((1, 3), (3, 1))
    pairs = [
        (core * size + i, core * size + (i ^ by[core][side]))
        for core in range(lax.axis_size("c"))
        for i in range(size)
    ]
    return lax.ppermute(t, ("c", "x"), pairs)


def on_device(q_resp, resp_kv, prompt_kv, d_out, resp_lengths):
    groups, own_rows, width = prompt_kv.shape
    ring = ("zl", "c", "zh", "y")
    copies = lax.axis_size(("zh", "y"))
    sent = jnp.broadcast_to(prompt_kv[:, None], (groups, copies, own_rows, width))
    own = exchange(sent.reshape(-1, own_rows, width), ring).reshape(-1, width)

    flat, resp_kind, prompt = (q_resp.shape, bf16), (resp_kv.shape, bf16), own.shape
    tall, stat_kind = (HEADS, HEAD, ROWS), ((HEADS, 16, ROWS), f32)
    parts = lambda n: [((HEADS, n * ROWS, ROWS), bf16), (tall, bf16), stat_kind]
    scores = lambda n: ((3, n * ROWS, ROWS), f32)
    sums = ((2, HEAD, 2 * ROWS), f32)
    self_low, self_out, self_stat = call(
        self_forward_kernel,
        "self_forward",
        parts(1),
        [
            pltpu.SMEM(resp_lengths.shape, jnp.int32),
            flat,
            resp_kind,
            ((ROWS, ROWS), f32),
            scores(1),
            *parts(1),
            pltpu.SemaphoreType.DMA((3,)),
            pltpu.SemaphoreType.DMA((3,)),
        ],
        [resp_lengths, q_resp, resp_kv],
        flops=1 << 33,
        in_hbm=True,
    )

    own, self_stat = lax.optimization_barrier((own, self_stat))
    own_k, own_v = own[:, :WIDTH], own[:, WIDTH:]
    one_k, three_v = to_neighbour(own_k, 0), to_neighbour(own_v, 1)
    one_v, three_k = to_neighbour(own_v, 0), to_neighbour(own_k, 1)
    far_k, far_v = to_neighbour(one_k, 1), to_neighbour(three_v, 0)
    next_ = [one_k, one_v, three_k, three_v]
    next_low, next_out, next_stat = call(
        next_forward_kernel, "next_forward", parts(3), [scores(3)], [q_resp, *next_, own]
    )
    half = lambda dtype: ((ROWS, WIDTH), dtype)
    out, dq, stat, dk, dv = call(
        opposite_kernel,
        "opposite",
        [(tall, bf16), (tall, f32), ((HEADS, 24, ROWS), f32), half(bf16), half(bf16)],
        [
            ((KV_HEADS, 2, HEAD, ROWS), f32),
            ((2, ROWS, ROWS), f32),
            ((4, ROWS, ROWS), bf16),
            ((4, ROWS, ROWS), f32),
        ],
        [q_resp, d_out, far_k, far_v, self_out, self_stat, next_out, next_stat],
    )
    dk, dv = to_neighbour(dk, 1), to_neighbour(dv, 0)
    dq, d_one_k, d_one_v, d_three_k, d_three_v = call(
        next_backward_kernel,
        "next_backward",
        [(tall, f32), half(f32), half(bf16), half(bf16), half(f32)],
        [sums, scores(2)],
        [q_resp, d_out, *next_, next_low, stat, dq],
        specs={6: pl.BlockSpec((HEADS, 2 * ROWS, ROWS), lambda i: (0, 0, 0))},
    )
    d_one_v, d_three_k = to_neighbour(d_one_v, 0), to_neighbour(d_three_k, 1)
    dk, dv, d_one_k, d_three_v = lax.optimization_barrier((dk, dv, d_one_k, d_three_v))
    d_one_k, d_three_v = added(d_one_k, dk), added(d_three_v, dv)
    d_one_k, d_three_v = lax.optimization_barrier((d_one_k, d_three_v))
    d_one_k, d_three_v = to_neighbour(d_one_k, 0), to_neighbour(d_three_v, 1)
    attn, dq, d_own, d_resp = call(
        near_backward_kernel,
        "near_backward",
        [flat, flat, (prompt, f32), resp_kind],
        [sums, scores(2)],
        [q_resp, d_out, own, resp_kv, next_low, self_low, stat, dq, out],
        specs={4: pl.BlockSpec((HEADS, ROWS, ROWS), lambda i: (0, 2, 0))},
    )
    came = (d_one_k, d_three_k, d_one_v, d_three_v)
    d_own, *came = lax.optimization_barrier((d_own, *came))
    keys = added(d_own[:, :WIDTH], came[0], came[1])
    vals = added(d_own[:, WIDTH:], came[2], came[3])
    total = jnp.concatenate([keys, vals], 1)
    total = exchange(total.reshape(-1, own_rows, width), ring)
    total = total.reshape(groups, copies, own_rows, width)
    d_prompt = jnp.sum(total.astype(f32), axis=1).astype(bf16)
    return attn, dq, d_resp, d_prompt


def solution(mesh):
    fine = Mesh(mesh.devices.reshape(4, 2, 2, 4, 4), ("zl", "c", "zh", "y", "x"))
    grp, seq = ("zl", "c"), ("zh", "y", "x")
    rows = P(grp, seq, None)
    prompt = P(None, grp + seq, None)
    return jax.shard_map(
        on_device,
        mesh=fine,
        in_specs=(rows, rows, prompt, rows, rows),
        out_specs=(rows, rows, rows, prompt),
        check_vma=False,
    )
```

```python
import functools

import jax
import jax.numpy as jnp
from jax import lax
from jax.experimental import pallas as pl
from jax.experimental.pallas import tpu as pltpu
from jax.sharding import Mesh
from jax.sharding import PartitionSpec as P

HEADS = 10
KV_HEADS = 2
HEAD = 128
REPEAT = HEADS // KV_HEADS
SCALE = HEAD ** (-0.5)
LOG2E = 1.4426950408889634
MASKED = -1e30
WIDTH = KV_HEADS * HEAD
ROWS = 256
bf16 = jnp.bfloat16
f32 = jnp.float32


def dot_nn(a, b):
    return lax.dot_general(a, b, (((1,), (0,)), ((), ())), preferred_element_type=f32)


def dot_nt(a, b):
    return lax.dot_general(a, b, (((1,), (1,)), ((), ())), preferred_element_type=f32)


def by_eights(op, t):
    return op(t.reshape(t.shape[0] // 8, 8, t.shape[1]), axis=0)


def of_keys(head):
    at = head // REPEAT * HEAD
    return slice(at, at + HEAD)


def of_vals(head):
    at = WIDTH + head // REPEAT * HEAD
    return slice(at, at + HEAD)


def of_head(head):
    return slice(head * HEAD, (head + 1) * HEAD)


def self_bias(lens_ref, rows):
    key = lax.broadcasted_iota(jnp.int32, (rows, rows), 0)
    row = lax.broadcasted_iota(jnp.int32, (rows, rows), 1)
    key_seg = jnp.zeros((rows, rows), jnp.int32)
    row_seg = jnp.zeros((rows, rows), jnp.int32)
    end = jnp.int32(0)
    for i in range(lens_ref.shape[-1]):
        end = end + lens_ref[0, 0, i]
        key_seg += (key >= end).astype(jnp.int32)
        row_seg += (row >= end).astype(jnp.int32)
    return jnp.where((key_seg == row_seg) & (key <= row), 0.0, MASKED).astype(f32)


def scaled(t, factor):
    return (t.astype(f32) * factor).astype(bf16)


def of_group(head):
    at = head // REPEAT * HEAD
    return slice(at, at + HEAD)


def start_all(copies, semaphores):
    started = []
    for i, (source, target) in enumerate(copies):
        started.append(pltpu.make_async_copy(source, target, semaphores.at[i]))
        started[-1].start()
    return started


def wait_all(copies):
    for copy in copies:
        copy.wait()


def halves(ref):
    return ref.at[:, :WIDTH], ref.at[:, WIDTH:]


def eight(row):
    return jnp.broadcast_to(row, (8, row.shape[1]))


def places_of(chunks):
    return [slice(i * ROWS, (i + 1) * ROWS) for i in range(len(chunks))]


def forward(q_ref, chunks, bias_ref, low_ref, out_ref, stat_ref, scores_ref):
    places = places_of(chunks)
    vals_t = [
        jnp.concatenate([v[:, of_group(g * REPEAT)].T for _, v in chunks], 1)
        for g in range(KV_HEADS)
    ]
    first = lax.broadcasted_iota(jnp.int32, (16, len(chunks) * ROWS), 0) == 0
    one_row = first.astype(f32).astype(bf16)
    vals_t = [jnp.concatenate([t, one_row], 0) for t in vals_t]
    tops = {}

    def score_pass(h):
        q_t = q_ref[0, :, of_head(h)].T
        top = None
        for at, (k, _) in zip(places, chunks):
            s = dot_nn(k[:, of_group(h)], q_t)
            if bias_ref is not None and at is places[-1]:
                s = s + bias_ref[...]
            scores_ref[h % 2, at] = s
            s = by_eights(jnp.max, s)
            top = s if top is None else jnp.maximum(top, s)
        tops[h] = jnp.max(top, axis=0, keepdims=True) * (SCALE * LOG2E)

    def weight_pass(h):
        for at in places:
            weights = jnp.exp2(scores_ref[h % 2, at] * (SCALE * LOG2E) - tops[h])
            low_ref[h, at] = weights.astype(bf16)
        out_t = dot_nn(vals_t[h // REPEAT], low_ref[h])
        stat_ref[h, 0:8] = eight(tops[h])
        stat_ref[h, 8:16] = out_t[HEAD : HEAD + 8]
        out_ref[h] = out_t[:HEAD].astype(bf16)

    score_pass(0)
    for h in range(HEADS):
        if h + 1 < HEADS:
            score_pass(h + 1)
        weight_pass(h)


def backward(q_ref, do_ref, chunks, lows, shares, stat_ref, acc, d_probs_ref, put_dq, put_sums):
    places = places_of(chunks)
    keys_t = [[k[:, of_group(g * REPEAT)].T for k, _ in chunks] for g in range(KV_HEADS)]
    d_outs = {}

    def d_probs_pass(h):
        d_outs[h] = do_ref[0, :, of_head(h)].T
        for at, (_, v) in zip(places, chunks):
            d_probs_ref[h % 2, at] = dot_nn(v[:, of_group(h)], d_outs[h])

    def add(h, j, at, new):
        acc[j, :, at] = new if h % REPEAT == 0 else acc[j, :, at] + new

    def gradient_pass(h):
        delta = stat_ref[h, 0:1]
        share = {at: stat_ref[h, at : at + 1] for at in set(shares)}
        do_scaled = {at: scaled(d_outs[h], t) for at, t in share.items()}
        q_t = q_ref[0, :, of_head(h)].T
        q_scaled = {at: scaled(q_t, t * SCALE) for at, t in share.items()}
        for at, low, which in zip(places, lows, shares):
            add(h, 1, at, dot_nt(do_scaled[which], low(h)))
        dq_t = {at: 0.0 for at in share}
        for at, low, which, k_t in zip(places, lows, shares, keys_t[h // REPEAT]):
            d_probs = d_probs_ref[h % 2, at] - delta
            d_scores = (low(h).astype(f32) * d_probs).astype(bf16)
            dq_t[which] = dq_t[which] + dot_nn(k_t, d_scores)
            add(h, 0, at, dot_nt(q_scaled[which], d_scores))
        put_dq(h, sum(dq_t[at] * (share[at] * SCALE) for at in sorted(share)))
        if h % REPEAT == REPEAT - 1:
            for j in range(2):
                put_sums(j, of_group(h), [acc[j, :, at].T for at in places])

    d_probs_pass(0)
    for h in range(HEADS):
        if h + 1 < HEADS:
            d_probs_pass(h + 1)
        gradient_pass(h)


def self_forward_kernel(
    lens_hbm, q_hbm, resp_hbm, low_hbm, out_hbm, stat_hbm,
    lens_ref, q_ref, resp_ref, bias_ref, scores_ref, low_ref, out_ref, stat_ref, arrived, left,
):
    arriving = start_all(((lens_hbm, lens_ref), (resp_hbm, resp_ref), (q_hbm, q_ref)), arrived)
    wait_all(arriving[:1])
    bias_ref[...] = self_bias(lens_ref, ROWS)
    wait_all(arriving[1:])
    chunks = [halves(resp_ref.at[0])]
    forward(q_ref, chunks, bias_ref, low_ref, out_ref, stat_ref, scores_ref)
    wait_all(start_all(((low_ref, low_hbm), (out_ref, out_hbm), (stat_ref, stat_hbm)), left))


def next_forward_kernel(
    q_ref, one_k, one_v, three_k, three_v, own_ref, low_ref, out_ref, stat_ref, scores_ref
):
    chunks = [(one_k, one_v), (three_k, three_v), halves(own_ref)]
    forward(q_ref, chunks, None, low_ref, out_ref, stat_ref, scores_ref)


def opposite_kernel(
    q_ref, do_ref, k_ref, v_ref, self_out_ref, self_stat_ref, next_out_ref, next_stat_ref,
    out_ref, dq_ref, stat_ref, dk_ref, dv_ref, acc, scores_ref, low_ref, d_probs_ref,
):
    heads = range(0, HEADS, REPEAT)
    keys_t = [k_ref[:, of_group(h)].T for h in heads]
    vals_t = [v_ref[:, of_group(h)].T for h in heads]
    state = [{} for _ in range(HEADS)]

    def score_pass(h):
        q_t = q_ref[0, :, of_head(h)].T
        s = dot_nn(k_ref[:, of_group(h)], q_t)
        scores_ref[h % 2] = s
        top = by_eights(jnp.max, s) * (SCALE * LOG2E)
        top = jnp.maximum(jnp.maximum(self_stat_ref[h, 0:8], next_stat_ref[h, 0:8]), top)
        state[h].update(q_t=q_t, top=jnp.max(top, axis=0, keepdims=True))

    def weight_pass(h):
        top = state[h]["top"]
        weights = jnp.exp2(scores_ref[h % 2] * (SCALE * LOG2E) - top)
        low = weights.astype(bf16)
        low_ref[h % 4] = low
        own = jnp.exp2(self_stat_ref[h, 0:1] - top)
        next_ = jnp.exp2(next_stat_ref[h, 0:1] - top)
        sums = by_eights(jnp.sum, weights)
        sums = sums + self_stat_ref[h, 8:16] * own + next_stat_ref[h, 8:16] * next_
        inverse = 1.0 / jnp.sum(sums, axis=0, keepdims=True)
        out_t = self_out_ref[h].astype(f32) * own + next_out_ref[h].astype(f32) * next_
        out_t = (out_t + dot_nn(vals_t[h // REPEAT], low)) * inverse
        do_t = do_ref[0, :, of_head(h)].T
        d_probs_ref[h % 4] = dot_nn(v_ref[:, of_group(h)], do_t)
        stat_ref[h, 8:16] = eight(inverse * own)
        stat_ref[h, 16:24] = eight(inverse * next_)
        state[h].update(inverse=inverse, do_t=do_t, out_t=out_t)

    def delta_pass(h):
        do_t, out_t = state[h]["do_t"], state[h]["out_t"]
        delta = jnp.sum(
            do_t.astype(f32) * out_t.astype(bf16).astype(f32), axis=0, keepdims=True
        )
        stat_ref[h, 0:8] = eight(delta)
        out_ref[h] = out_t.astype(bf16)
        state[h]["delta"] = delta
        add(h, 1, dot_nt(scaled(do_t, state[h]["inverse"]), low_ref[h % 4]))

    def add(h, j, new):
        at = (h // REPEAT, j)
        acc[at] = new if h % REPEAT == 0 else acc[at] + new

    def gradient_pass(h):
        inverse = state[h]["inverse"]
        d_probs = d_probs_ref[h % 4] - state[h]["delta"]
        d_scores = (low_ref[h % 4].astype(f32) * d_probs).astype(bf16)
        dq_ref[h] = dot_nn(keys_t[h // REPEAT], d_scores) * (inverse * SCALE)
        add(h, 0, dot_nt(scaled(state[h]["q_t"], inverse * SCALE), d_scores))
        if h % REPEAT == REPEAT - 1:
            dk_ref[:, of_group(h)] = acc[h // REPEAT, 0].T.astype(bf16)
            dv_ref[:, of_group(h)] = acc[h // REPEAT, 1].T.astype(bf16)

    passes = (gradient_pass, delta_pass, weight_pass, score_pass)
    for step in range(1 - len(passes), HEADS):
        for lag in (1, 3, 0, 2):
            if 0 <= step + lag < HEADS:
                passes[lag](step + lag)


def next_backward_kernel(
    q_ref, do_ref, one_k, one_v, three_k, three_v, low_ref, stat_ref, dq_part_ref,
    dq_ref, d_one_k, d_one_v, d_three_k, d_three_v, acc, d_probs_ref,
):
    def put_dq(h, dq_t):
        dq_ref[h] = dq_part_ref[h] + dq_t

    def put_sums(j, cols, sums):
        for t, ref in zip(sums, ((d_one_k, d_three_k), (d_one_v, d_three_v))[j]):
            ref[:, cols] = t.astype(ref.dtype)

    chunks = [(one_k, one_v), (three_k, three_v)]
    lows = [lambda h, at=at: low_ref[h, at] for at in places_of(chunks)]
    backward(q_ref, do_ref, chunks, lows, [16, 16], stat_ref, acc, d_probs_ref, put_dq, put_sums)


def near_backward_kernel(
    q_ref, do_ref, own_ref, resp_ref, low_ref, self_low_ref, stat_ref, dq_part_ref, out_ref,
    attn_ref, dq_ref, d_own_ref, d_resp_ref, acc, d_probs_ref,
):
    def put_dq(h, dq_t):
        dq_ref[0, :, of_head(h)] = (dq_part_ref[h] + dq_t).T.astype(bf16)
        attn_ref[0, :, of_head(h)] = out_ref[h].T

    def put_sums(j, cols, sums):
        cols = slice(j * WIDTH + cols.start, j * WIDTH + cols.stop)
        d_own_ref[:, cols] = sums[0]
        d_resp_ref[0, :, cols] = sums[1].astype(bf16)

    chunks = [halves(own_ref), halves(resp_ref.at[0])]
    lows = [lambda h: low_ref[h], lambda h: self_low_ref[h]]
    backward(q_ref, do_ref, chunks, lows, [16, 8], stat_ref, acc, d_probs_ref, put_dq, put_sums)


def whole(shape):
    return pl.BlockSpec(shape, lambda i: (0,) * len(shape))


def call(kernel, name, outs, scratch, args, flops=ROWS, in_hbm=False, specs={}):
    hbm = pl.BlockSpec(memory_space=pltpu.HBM)
    if in_hbm:
        args = [pltpu.with_memory_space_constraint(t, pltpu.HBM) for t in args]
    return pl.pallas_call(
        kernel,
        grid=(1,),
        in_specs=[hbm if in_hbm else specs.get(i, whole(t.shape)) for i, t in enumerate(args)],
        out_specs=[hbm if in_hbm else whole(shape) for shape, _ in outs],
        out_shape=[
            pltpu.HBM(shape, dtype) if in_hbm else jax.ShapeDtypeStruct(shape, dtype)
            for shape, dtype in outs
        ],
        scratch_shapes=[pltpu.VMEM(*t) if isinstance(t, tuple) else t for t in scratch],
        compiler_params=pltpu.CompilerParams(vmem_limit_bytes=30 << 20),
        cost_estimate=pl.CostEstimate(flops=flops, bytes_accessed=ROWS, transcendentals=0),
        name=name,
    )(*args)


def added(*terms):
    return sum(t.astype(f32) for t in terms).astype(bf16)


def exchange(t, axes):
    return lax.all_to_all(t, axes, split_axis=0, concat_axis=0, tiled=True)


def to_neighbour(t, side):
    size = lax.axis_size("x")
    by = ((1, 3), (3, 1))
    pairs = [
        (core * size + i, core * size + (i ^ by[core][side]))
        for core in range(lax.axis_size("c"))
        for i in range(size)
    ]
    return lax.ppermute(t, ("c", "x"), pairs)


def on_device(q_resp, resp_kv, prompt_kv, d_out, resp_lengths):
    groups, own_rows, width = prompt_kv.shape
    ring = ("zl", "c", "zh", "y")
    copies = lax.axis_size(("zh", "y"))
    sent = jnp.broadcast_to(prompt_kv[:, None], (groups, copies, own_rows, width))
    own = exchange(sent.reshape(-1, own_rows, width), ring).reshape(-1, width)

    flat, resp_kind, prompt = (q_resp.shape, bf16), (resp_kv.shape, bf16), own.shape
    tall, stat_kind = (HEADS, HEAD, ROWS), ((HEADS, 16, ROWS), f32)
    parts = lambda n: [((HEADS, n * ROWS, ROWS), bf16), (tall, bf16), stat_kind]
    scores = lambda n: ((2, n * ROWS, ROWS), f32)
    sums = ((2, HEAD, 2 * ROWS), f32)
    self_low, self_out, self_stat = call(
        self_forward_kernel,
        "self_forward",
        parts(1),
        [
            pltpu.SMEM(resp_lengths.shape, jnp.int32),
            flat,
            resp_kind,
            ((ROWS, ROWS), f32),
            scores(1),
            *parts(1),
            pltpu.SemaphoreType.DMA((3,)),
            pltpu.SemaphoreType.DMA((3,)),
        ],
        [resp_lengths, q_resp, resp_kv],
        flops=1 << 33,
        in_hbm=True,
    )

    own, self_stat = lax.optimization_barrier((own, self_stat))
    own_k, own_v = own[:, :WIDTH], own[:, WIDTH:]
    one_k, three_v = to_neighbour(own_k, 0), to_neighbour(own_v, 1)
    one_v, three_k = to_neighbour(own_v, 0), to_neighbour(own_k, 1)
    far_k, far_v = to_neighbour(one_k, 1), to_neighbour(three_v, 0)
    next_ = [one_k, one_v, three_k, three_v]
    next_low, next_out, next_stat = call(
        next_forward_kernel, "next_forward", parts(3), [scores(3)], [q_resp, *next_, own]
    )
    half = lambda dtype: ((ROWS, WIDTH), dtype)
    out, dq, stat, dk, dv = call(
        opposite_kernel,
        "opposite",
        [(tall, bf16), (tall, f32), ((HEADS, 24, ROWS), f32), half(bf16), half(bf16)],
        [
            ((KV_HEADS, 2, HEAD, ROWS), f32),
            ((2, ROWS, ROWS), f32),
            ((4, ROWS, ROWS), bf16),
            ((4, ROWS, ROWS), f32),
        ],
        [q_resp, d_out, far_k, far_v, self_out, self_stat, next_out, next_stat],
    )
    dk, dv = to_neighbour(dk, 1), to_neighbour(dv, 0)
    dq, d_one_k, d_one_v, d_three_k, d_three_v = call(
        next_backward_kernel,
        "next_backward",
        [(tall, f32), half(f32), half(bf16), half(bf16), half(f32)],
        [sums, scores(2)],
        [q_resp, d_out, *next_, next_low, stat, dq],
        specs={6: pl.BlockSpec((HEADS, 2 * ROWS, ROWS), lambda i: (0, 0, 0))},
    )
    d_one_v, d_three_k = to_neighbour(d_one_v, 0), to_neighbour(d_three_k, 1)
    dk, dv, d_one_k, d_three_v = lax.optimization_barrier((dk, dv, d_one_k, d_three_v))
    d_one_k, d_three_v = added(d_one_k, dk), added(d_three_v, dv)
    d_one_k, d_three_v = lax.optimization_barrier((d_one_k, d_three_v))
    d_one_k, d_three_v = to_neighbour(d_one_k, 0), to_neighbour(d_three_v, 1)
    attn, dq, d_own, d_resp = call(
        near_backward_kernel,
        "near_backward",
        [flat, flat, (prompt, f32), resp_kind],
        [sums, scores(2)],
        [q_resp, d_out, own, resp_kv, next_low, self_low, stat, dq, out],
        specs={4: pl.BlockSpec((HEADS, ROWS, ROWS), lambda i: (0, 2, 0))},
    )
    came = (d_one_k, d_three_k, d_one_v, d_three_v)
    d_own, *came = lax.optimization_barrier((d_own, *came))
    keys = added(d_own[:, :WIDTH], came[0], came[1])
    vals = added(d_own[:, WIDTH:], came[2], came[3])
    total = jnp.concatenate([keys, vals], 1)
    total = exchange(total.reshape(-1, own_rows, width), ring)
    total = total.reshape(groups, copies, own_rows, width)
    d_prompt = jnp.sum(total.astype(f32), axis=1).astype(bf16)
    return attn, dq, d_resp, d_prompt


def solution(mesh):
    fine = Mesh(mesh.devices.reshape(4, 2, 2, 4, 4), ("zl", "c", "zh", "y", "x"))
    grp, seq = ("zl", "c"), ("zh", "y", "x")
    rows = P(grp, seq, None)
    prompt = P(None, grp + seq, None)
    return jax.shard_map(
        on_device,
        mesh=fine,
        in_specs=(rows, rows, prompt, rows, rows),
        out_specs=(rows, rows, rows, prompt),
        check_vma=False,
    )
```
